256 devices in a mesh: seq: 16 (over y_hi, x, core), mp: 16 (over z, y_lo).
Axes of the slice: x: 4, y: 4 (y_hi: 2, y_lo: 2; y = y_hi * 2 + y_lo), z: 8, core: 2. Of those that a mesh axis runs over, the one named last changes fastest.
Arguments:
- query: bfloat16 [8192, 8192], P('seq', 'mp'), may hold values from -240 to 240
- residual: float32 [8192, 8192], P('seq', 'mp'), may hold values from -6 to 6
- nbr_ids: int32 [128, 2, 128], P('seq'), may hold values from 0 to 65535
- embed: bfloat16 [65536, 896], P('mp'), may hold values from -6 to 6
- enc_gain: float32 [896], replicated, may hold values from 0.1 to 1.9
- w_key: bfloat16 [896, 8192], P(None, 'mp'), may hold values from -0.1875 to 0.1875
- w_value: bfloat16 [896, 8192], P(None, 'mp'), may hold values from -0.1875 to 0.1875
- w_out: bfloat16 [8192, 8192], P(('mp', 'seq')), may hold values from -0.0625 to 0.0625
Outputs:
- mixed: float32 [8192, 8192], P('seq', 'mp')
The draws below stay inside these ranges and needn't reach their ends.
All inputs are finite; a program needn't handle non-finite values.
Results may differ from the reference program's by a relative error of at most 0.011.
Values may be sent and summed in bfloat16 or wider, within the bound.
No kernel may reach another device: no remote copies, remote signals or barrier semaphores. Data moves between devices by JAX's collectives and lax.ppermute only.
A program may use at most 128 MiB of HBM per device.

```python
import jax
import jax.numpy as jnp
from jax import lax

D = 8192
HEADS = 64
HD = 128
DE = 896
VOCAB = 65536
SPAN = 64
NBRS = 2
NLEN = 128
TOKENS = 8192
SPANS = 128


def draw_query(key, part):
    key = jax.random.fold_in(key, 11)
    base = jnp.clip(jax.random.normal(jax.random.fold_in(key, 1), (TOKENS, D), jnp.float32), -6.0, 6.0)
    return base.astype(jnp.bfloat16)


def plant(drawn, rng, smallest, largest):
    spot = [jax.random.randint(jax.random.fold_in(rng, axis), (), 0, length) for axis, length in enumerate(drawn.shape)]
    main_axis = drawn.shape.index(max(drawn.shape))
    beside = spot[:main_axis] + [(spot[main_axis] + 1) % drawn.shape[main_axis]] + spot[main_axis + 1:]
    return drawn.at[tuple(spot)].set(smallest).at[tuple(beside)].set(largest)


def shard_levels(stream_key, extent, shards, least, largest):
    gain = 1.0
    for axis_at, blocks in shards:
        steps = jax.random.uniform(jax.random.fold_in(jax.random.fold_in(stream_key, 6), axis_at), (blocks,), jnp.float32, least / len(shards), largest / len(shards))
        gain = gain * jnp.repeat(jnp.exp(steps), extent[axis_at] // blocks).reshape((-1,) + (1,) * (len(extent) - 1 - axis_at))
    return gain


def centred(key, extent, width, limit, split=(), kind=jnp.bfloat16):
    drawn = jax.random.normal(key, extent, jnp.float32) * width
    if len(split) > 0:
        drawn = shard_levels(key, extent, split, -0.22, 0.18) * drawn
    return jnp.clip(drawn, min=-limit, max=limit).astype(kind)


def setup_inputs(seed: int = 0) -> dict:
    key_list = jax.random.split(jax.random.key(seed), 9)
    return {
        "query": draw_query(jax.random.fold_in(key_list[8], 71), 0),
        "residual": centred(key_list[1], (TOKENS, D), 1.0, 6.0, ((0, 16), (1, 16)), jnp.float32),
        "nbr_ids": plant(jax.random.randint(key_list[2], (SPANS, NBRS, NLEN), 0, VOCAB), jax.random.fold_in(key_list[2], 1), 0, VOCAB - 1).astype(jnp.int32),
        "embed": centred(key_list[3], (VOCAB, DE), 1.0, 6.0, ((0, 16),)),
        "enc_gain": jnp.clip(1.0 + 0.18 * jax.random.normal(key_list[4], (DE,), jnp.float32), 0.1, 1.9),
        "w_key": centred(key_list[5], (DE, D), DE ** -0.5, 0.1875, ((1, 16),)),
        "w_value": centred(key_list[6], (DE, D), DE ** -0.5, 0.1875, ((1, 16),)),
        "w_out": centred(key_list[7], (D, D), D ** -0.5, 0.0625, ((0, 256),)),
    }


def encode(ids, embed, enc_gain, w_key, w_value):
    emb = jnp.take(embed, ids.reshape(-1), axis=0)
    wide = emb.astype(jnp.float32)
    power = lax.optimization_barrier(jnp.mean(wide * wide, axis=-1, keepdims=True))
    enc = (wide * lax.rsqrt(power + 1e-06) * enc_gain).astype(jnp.bfloat16)
    keys = jnp.dot(enc, w_key, preferred_element_type=jnp.float32).astype(jnp.bfloat16)
    values = jnp.dot(enc, w_value, preferred_element_type=jnp.float32).astype(jnp.bfloat16)
    return (keys, values)

def reference(query, residual, nbr_ids, embed, enc_gain, w_key, w_value, w_out):
    padded = jnp.concatenate([jnp.zeros((1, D), jnp.bfloat16), query, jnp.zeros((SPAN - 1, D), jnp.bfloat16)], axis=0)

    def group(index):
        rows = lax.dynamic_slice_in_dim(padded, index * SPAN, SPAN, 0)
        span = jnp.maximum(index - 1, 0).astype(jnp.int32)
        ids = lax.dynamic_index_in_dim(nbr_ids, span, 0, keepdims=False)
        keys, values = encode(ids, embed, enc_gain, w_key, w_value)
        live = (index > 0).astype(jnp.bfloat16)
        keys = keys * live
        values = values * live
        qq = rows.reshape(SPAN, HEADS, HD).astype(jnp.float32)
        kk = keys.reshape(NBRS * NLEN, HEADS, HD).astype(jnp.float32)
        vv = values.reshape(NBRS * NLEN, HEADS, HD).astype(jnp.float32)
        scores = jnp.einsum('qhd,khd->hqk', qq, kk) * HD ** (-0.5)
        weights = jax.nn.softmax(scores, axis=-1).astype(jnp.bfloat16)
        attn = jnp.einsum('hqk,khd->qhd', weights.astype(jnp.float32), vv)
        return attn.astype(jnp.bfloat16).reshape(SPAN, D)
    stacked = lax.map(group, jnp.arange(SPANS + 1, dtype=jnp.int32))
    attn = stacked.reshape((SPANS + 1) * SPAN, D)[1:1 + TOKENS]
    return residual + jnp.dot(attn, w_out, preferred_element_type=jnp.float32)
```

```python
import functools

import jax
import jax.numpy as jnp
from jax import lax
from jax.experimental import pallas as pl
from jax.experimental.pallas import tpu as pltpu
from jax.sharding import Mesh
from jax.sharding import PartitionSpec as P

HD = 128
SPAN = 64
KEYS = 256
ROOM = 112
SEQ = ("yhi", "x", "core")
MP = ("z", "ylo")
SWAP = [(0, 1), (1, 0)]


def normed(rows, gain):
    wide = rows.astype(jnp.float32)
    power = jnp.mean(wide * wide, axis=-1, keepdims=True)
    return (wide * lax.rsqrt(power + 1e-06) * gain).astype(jnp.bfloat16)


def span_attention(enc, wk, wv, q, o):
    keys = jnp.dot(enc, wk[...], preferred_element_type=jnp.float32).astype(jnp.bfloat16)
    values = jnp.dot(enc, wv[...], preferred_element_type=jnp.float32).astype(jnp.bfloat16)
    for head in range(q.shape[1] // HD):
        at = slice(head * HD, (head + 1) * HD)
        scores = lax.dot_general(
            q[:, at], keys[:, at], (((1,), (1,)), ((), ())), preferred_element_type=jnp.float32
        ) * HD ** (-0.5)
        shifted = jnp.exp(scores - jnp.max(scores, axis=-1, keepdims=True))
        weights = (shifted / jnp.sum(shifted, axis=-1, keepdims=True)).astype(jnp.bfloat16)
        o[:, at] = jnp.dot(weights, values[:, at], preferred_element_type=jnp.float32).astype(jnp.bfloat16)


def attend(enc_ref, wk, wv, q, o):
    span_attention(enc_ref[...], wk, wv, q, o)


def attention(enc, wk, wv, q):
    spans = enc.shape[0] // KEYS
    depth, width = wk.shape
    whole = pl.BlockSpec((depth, width), lambda i: (0, 0))
    tokens = pl.BlockSpec((SPAN, width), lambda i: (i, 0))
    return pl.pallas_call(
        attend,
        grid=(spans,),
        in_specs=[pl.BlockSpec((KEYS, depth), lambda i: (i, 0)), whole, whole, tokens],
        out_specs=tokens,
        out_shape=jax.ShapeDtypeStruct((spans * SPAN, width), jnp.bfloat16),
        compiler_params=pltpu.CompilerParams(vmem_limit_bytes=24 * 2**20),
        cost_estimate=pl.CostEstimate(
            flops=spans * KEYS * depth * width * 4, bytes_accessed=6 * 2**20, transcendentals=spans * 2**16
        ),
    )(enc, wk, wv, q)


def panel_rows(w_ref, side):
    half, width = w_ref.shape[1] // 2, w_ref.shape[2]
    return w_ref[:, side * half : (side + 1) * half, :].reshape(width, width)


def project(at_ref, *refs):
    blocks = refs[:-6]
    w_ref, own_ref, par_ref, here, total, sems = refs[-6:]
    step = pl.program_id(0)
    copies = [pltpu.make_async_copy(block, here.at[i], sems.at[i]) for i, block in enumerate(blocks)]

    @pl.when(step == 0)
    def _():
        for copy in copies:
            copy.start()

    for i, copy in enumerate(copies):

        @pl.when(step == i)
        def _():
            copy.wait()
            for side in range(2):
                w = panel_rows(w_ref, side)
                done = jnp.dot(here[i], w, preferred_element_type=jnp.float32)
                if i > 0:
                    done = done + total[side]
                if i < len(copies) - 1:
                    total[side] = done
                elif side == 0:
                    own_ref[...] = done
                else:
                    par_ref[...] = done.astype(jnp.bfloat16)


def projected(at, blocks, panel):
    steps = len(blocks)
    tokens, width = blocks[0].shape
    seqs, sides = panel.shape[0], 2
    rows = sides * width // seqs
    whole = pl.BlockSpec((tokens, width), lambda i, at: (0, 0))
    return pl.pallas_call(
        project,
        grid_spec=pltpu.PrefetchScalarGridSpec(
            num_scalar_prefetch=1,
            grid=(steps,),
            in_specs=[pl.BlockSpec(memory_space=pl.ANY)] * steps
            + [pl.BlockSpec((seqs, rows, width), lambda i, at: (0, at[i], 0))],
            out_specs=[whole, whole],
            scratch_shapes=[
                pltpu.VMEM((steps, tokens, width), jnp.bfloat16),
                pltpu.VMEM((sides, tokens, width), jnp.float32),
                pltpu.SemaphoreType.DMA((steps,)),
            ],
        ),
        out_shape=[
            jax.ShapeDtypeStruct((tokens, width), jnp.float32),
            jax.ShapeDtypeStruct((tokens, width), jnp.bfloat16),
        ],
        compiler_params=pltpu.CompilerParams(vmem_limit_bytes=40 * 2**20),
        cost_estimate=pl.CostEstimate(
            flops=4 * steps * tokens * width * width, bytes_accessed=12 * 2**20, transcendentals=0
        ),
    )(at, *blocks, panel)


def half_rows(ids, embed, y):
    zs = lax.axis_size("z")
    block = embed.shape[0]
    each = ids.size // 2 // zs
    order = ids.reshape(2, zs, each).transpose(1, 0, 2).reshape(-1)
    local = order - lax.axis_index(MP) * block
    inside = jnp.logical_and(local >= 0, local < block)
    picked = jnp.take(embed, jnp.clip(local, 0, block - 1), axis=0, mode="clip")
    picked = jnp.where(inside[:, None], picked, jnp.zeros_like(picked))
    part = lax.psum_scatter(picked, "z", scatter_dimension=0, tiled=True).reshape(2, each, -1)
    kept = lax.dynamic_index_in_dim(part, y, 0, keepdims=False)
    sent = lax.dynamic_index_in_dim(part, 1 - y, 0, keepdims=False)
    rows = kept + lax.ppermute(sent, "ylo", SWAP)
    return lax.all_gather(rows, "z", axis=0, tiled=True)


def choose(where_ref, ids_ref, slots_ref, *, block):
    me, y = where_ref[0], where_ref[1]
    rows, lanes = ids_ref.shape
    local = ids_ref[...] - me * block
    mine = jnp.logical_and(local >= 0, local < block)
    hot = mine.astype(jnp.float32)
    upper = (
        lax.broadcasted_iota(jnp.int32, (lanes, lanes), 0) < lax.broadcasted_iota(jnp.int32, (lanes, lanes), 1)
    ).astype(jnp.bfloat16)
    before = jnp.dot(hot.astype(jnp.bfloat16), upper, preferred_element_type=jnp.float32)
    many = jnp.sum(hot, axis=1, keepdims=True)
    ranks = jnp.concatenate([before] * (lanes // rows), axis=0).T
    locals_ = jnp.concatenate([jnp.where(mine, local, -1).astype(jnp.float32)] * (lanes // rows), axis=0).T
    placef = lax.broadcasted_iota(jnp.int32, (lanes, lanes), 1).astype(jnp.float32)
    each = rows // 2
    for half in range(2):
        total = jnp.zeros((lanes, lanes), jnp.float32)
        seen = jnp.zeros((1, 1), jnp.float32)
        for row in range(half * each, half * each + each):
            column = locals_[:, row : row + 1]
            chosen = jnp.logical_and(ranks[:, row : row + 1] + seen == placef, column >= 0)
            total = total + jnp.where(chosen, column, 0.0)
            seen = seen + many[row : row + 1, :]
        slots = jnp.broadcast_to(jnp.sum(total, axis=0, keepdims=True), (8, lanes)).astype(jnp.int32)
        slots_ref[pl.ds(pl.multiple_of((half ^ y) * 8, 8), 8), :] = slots


def chosen_rows(ids, where, block):
    vmem = pl.BlockSpec(memory_space=pltpu.VMEM)
    return pl.pallas_call(
        functools.partial(choose, block=block),
        in_specs=[pl.BlockSpec(memory_space=pltpu.SMEM), vmem],
        out_specs=vmem,
        out_shape=jax.ShapeDtypeStruct((16, ids.shape[1]), jnp.int32),
        compiler_params=pltpu.CompilerParams(vmem_limit_bytes=8 * 2**20),
        cost_estimate=pl.CostEstimate(flops=2**24, bytes_accessed=2**14, transcendentals=0),
    )(where, ids)


def plan(where_ref, ids_ref, pos_ref, over_ref, *, block, room):
    y, z = where_ref[1], where_ref[2]
    rows, lanes = ids_ref.shape
    each = rows // 2
    lane = lax.broadcasted_iota(jnp.int32, (1, lanes), 1)
    base = (((z - (lane >> 1)) & 7) * (2 * room) + jnp.where((lane & 1) == y, 0, room)).astype(jnp.float32)
    lower = (
        lax.broadcasted_iota(jnp.int32, (lanes, lanes), 0) > lax.broadcasted_iota(jnp.int32, (lanes, lanes), 1)
    ).astype(jnp.bfloat16)
    place = lax.broadcasted_iota(jnp.int32, (lanes, lanes), 1)
    most = jnp.zeros((1, lanes), jnp.float32)
    for side in range(2):
        half = y if side == 0 else 1 - y
        owners = ids_ref[pl.ds(pl.multiple_of(half * each, each), each), :] // block
        columns = jnp.concatenate([owners.astype(jnp.float32)] * (lanes // each), axis=0).T
        seen = jnp.zeros((1, lanes), jnp.float32)
        for row in range(each):
            hot = (columns[:, row : row + 1].astype(jnp.int32) == place).astype(jnp.float32)
            if side == 0:
                before = jnp.dot(lower, hot.astype(jnp.bfloat16), preferred_element_type=jnp.float32) + seen
                pos = jnp.sum(hot * (before + base), axis=1, keepdims=True)
                pos_ref[row * lanes : (row + 1) * lanes, :] = jnp.broadcast_to(pos, (lanes, lanes)).astype(jnp.int32)
            seen = seen + jnp.sum(hot, axis=0, keepdims=True)
        most = jnp.maximum(most, seen)
    over = jnp.max((most > room).astype(jnp.float32), axis=1, keepdims=True)
    over_ref[...] = jnp.broadcast_to(over, over_ref.shape).astype(over_ref.dtype)


def planned(ids, where, block, room, width):
    lanes = ids.shape[1]
    vmem = pl.BlockSpec(memory_space=pltpu.VMEM)
    return pl.pallas_call(
        functools.partial(plan, block=block, room=room),
        in_specs=[pl.BlockSpec(memory_space=pltpu.SMEM), vmem],
        out_specs=[vmem, vmem],
        out_shape=[
            jax.ShapeDtypeStruct((ids.size // 2, lanes), jnp.int32),
            jax.ShapeDtypeStruct((16, width), jnp.bfloat16),
        ],
        compiler_params=pltpu.CompilerParams(vmem_limit_bytes=16 * 2**20),
        cost_estimate=pl.CostEstimate(flops=2**27, bytes_accessed=2**20, transcendentals=0),
    )(where, ids)


def attend_from(tables, *refs):
    parts = refs[:tables]
    pos_ref, gain_ref, wk, wv, q, o, enc_ref, table = refs[tables:]
    room = parts[0].shape[0]

    @pl.when(pl.program_id(0) == 0)
    def _():
        for i, part in enumerate(parts):
            table[i * room : (i + 1) * room, :] = part[...]

    pos = pos_ref[...]
    lanes = pos.shape[1]
    lane = lax.broadcasted_iota(jnp.int32, pos.shape, 1)
    hot = jnp.concatenate(
        [(pos == lane + k * lanes).astype(jnp.bfloat16) for k in range(table.shape[0] // lanes)], axis=1
    )
    enc = normed(jnp.dot(hot, table[...], preferred_element_type=jnp.float32), gain_ref[...])
    enc_ref[...] = enc
    span_attention(enc, wk, wv, q, o)


def attention_from(parts, pos, gain, wk, wv, q):
    spans = pos.shape[0] // KEYS
    room, depth = parts[0].shape
    width = wk.shape[1]
    whole = pl.BlockSpec((depth, width), lambda i: (0, 0))
    tokens = pl.BlockSpec((SPAN, width), lambda i: (i, 0))
    span = pl.BlockSpec((KEYS, depth), lambda i: (i, 0))
    return pl.pallas_call(
        functools.partial(attend_from, len(parts)),
        grid=(spans,),
        in_specs=[pl.BlockSpec((room, depth), lambda i: (0, 0))] * len(parts)
        + [
            pl.BlockSpec((KEYS, pos.shape[1]), lambda i: (i, 0)),
            pl.BlockSpec((1, depth), lambda i: (0, 0)),
            whole, whole, tokens,
        ],
        out_specs=[tokens, span],
        out_shape=[
            jax.ShapeDtypeStruct((spans * SPAN, width), jnp.bfloat16),
            jax.ShapeDtypeStruct((spans * KEYS, depth), jnp.bfloat16),
        ],
        scratch_shapes=[pltpu.VMEM((len(parts) * room, depth), jnp.bfloat16)],
        compiler_params=pltpu.CompilerParams(vmem_limit_bytes=48 * 2**20),
        cost_estimate=pl.CostEstimate(
            flops=spans * KEYS * depth * width * 8, bytes_accessed=12 * 2**20, transcendentals=spans * 2**17
        ),
    )(*parts, pos, gain.reshape(1, -1), wk, wv, q)


def regroup(y_ref, w_ref, out_ref):
    pieces, sides, _, width = out_ref.shape
    for piece in range(pieces):
        for side in range(sides):
            start = pl.multiple_of((piece * sides + (side ^ y_ref[0])) * width, width)
            out_ref[piece, side] = w_ref[:, pl.ds(start, width)]


def regrouped(y, w, pieces, width):
    vmem = pl.BlockSpec(memory_space=pltpu.VMEM)
    return pl.pallas_call(
        regroup,
        in_specs=[pl.BlockSpec(memory_space=pltpu.SMEM), vmem],
        out_specs=vmem,
        out_shape=jax.ShapeDtypeStruct((pieces, 2, w.shape[0], width), w.dtype),
        compiler_params=pltpu.CompilerParams(vmem_limit_bytes=8 * 2**20),
        cost_estimate=pl.CostEstimate(flops=0, bytes_accessed=2 * w.size * 2, transcendentals=0),
    )(y.reshape(1), w)


def gather_z(x):
    n = lax.axis_size("z")
    blocks = lax.all_gather(x, "z")
    z = lax.axis_index("z")
    return [lax.dynamic_index_in_dim(blocks, lax.rem(z + n - d, n), 0, keepdims=False) for d in range(n)]


def hop(x, axis, by):
    n = lax.axis_size(axis)
    return lax.ppermute(x, axis, [(i, (i + by) % n) for i in range(n)])


def half_round(x):
    right, left = [x], [x]
    for _ in range(lax.axis_size("z") // 2 - 1):
        right.append(hop(right[-1], "z", 1))
        left.append(hop(left[-1], "z", -1))
    return right, left


def round_z(x, last):
    right, left = half_round(x)
    across = hop(right[-1], "z", 1) if last > 0 else hop(left[-1], "z", -1)
    return [*right, across, *left[:0:-1]]


def outputs(y, a_own, a_par, panel, slow):
    z = lax.axis_index("z")
    seqs = lax.axis_size(SEQ)
    a_rest = lax.ppermute(a_par, "ylo", SWAP)
    zs = lax.axis_size("z")
    if slow:
        near, far = gather_z(a_own), gather_z(a_rest)
    else:
        a_rest, _ = lax.optimization_barrier((a_rest, a_own))
        near, far = round_z(a_own, 1), round_z(a_rest, -1)
    order = (0, 1, zs - 1, 2, zs - 2, 3, zs - 3, zs // 2)
    at = jnp.stack([lax.rem(z + zs - d, zs) for d in order])
    own1, par1 = projected(at, [near[d] for d in order], panel)
    if not slow:
        far[zs // 2], own1, par1 = lax.optimization_barrier((far[zs // 2], own1, par1))
    other1 = lax.ppermute(par1, "ylo", SWAP)
    own2, par2 = projected(at, [far[d] for d in order], panel)
    other2 = lax.ppermute(par2, "ylo", SWAP)
    end = slice(own1.shape[0] - SPAN, None)
    onward = [(2 * i + side, 2 * i + 2 + side) for i in range(seqs - 1) for side in range(2)]
    across = [(2 * i + side, 2 * i + 3 - side) for i in range(seqs - 1) for side in range(2)]
    end_own = jnp.where(y == 1, own1[end], own2[end])
    end_par = jnp.where(y == 1, par1[end], par2[end])
    before = lax.ppermute(end_own, SEQ + ("ylo",), onward)
    before += lax.ppermute(end_par, SEQ + ("ylo",), across).astype(jnp.float32)
    first = own1 + other2.astype(jnp.float32)
    second = own2 + other1.astype(jnp.float32)
    return jnp.where(y == 0, first, second), jnp.where(y == 0, second, first), before


def finish(residual, first, second, before):
    moved = jnp.concatenate([before[1:], first, second[: second.shape[0] - SPAN + 1]], axis=0)
    return residual + moved


def per_device(query, residual, nbr_ids, embed, enc_gain, w_key, w_value, w_out):
    tokens, width = query.shape
    half = tokens // 2
    y = lax.axis_index("ylo")
    z = lax.axis_index("z")
    core = lax.axis_index("core")
    zs = lax.axis_size("z")
    seqs = lax.axis_size(SEQ)

    mine = lax.all_to_all(regrouped(y, w_out, zs, width), "z", 0, 0, tiled=True)

    where = jnp.stack([lax.axis_index(MP), y, z]).astype(jnp.int32)
    ids = nbr_ids.reshape(-1, nbr_ids.shape[-1])
    slots = chosen_rows(ids, where, embed.shape[0])
    chosen = jnp.concatenate([slots[0, :ROOM], slots[8, :ROOM]])
    picked = embed.at[chosen].get(mode="promise_in_bounds")
    near = round_z(picked[:ROOM], 1)
    got = lax.ppermute(picked[ROOM:], "ylo", SWAP)
    far = round_z(got, -1)
    parts = [part for pair in zip(near, far) for part in pair]

    ids, _ = lax.optimization_barrier((ids, got))
    pos, over = planned(ids, where, embed.shape[0], ROOM, width)
    mine = jnp.concatenate([mine.reshape(-1, width), over], axis=0)
    mine, _ = lax.optimization_barrier((mine, near[1]))
    panel = lax.all_gather(mine, SEQ, axis=0, tiled=False)

    sent = jnp.where(core == 0, w_key, w_value)
    sent, _ = lax.optimization_barrier((sent, got))
    wgot = lax.ppermute(sent, "ylo", SWAP)

    query, _ = lax.optimization_barrier((query, (near[2], near[6])))
    following = lax.ppermute(query[:SPAN], SEQ, [(i + 1, i) for i in range(seqs - 1)])
    moved = jnp.concatenate([query[SPAN - 1 :], following[: SPAN - 1]], axis=0).reshape(2, half, width)
    q_own = lax.dynamic_index_in_dim(moved, y, 0, keepdims=False)
    q_par = lax.ppermute(lax.dynamic_index_in_dim(moved, 1 - y, 0, keepdims=False), "ylo", SWAP)
    wgot, _ = lax.optimization_barrier((wgot, (near[3], near[5], far[3], far[5])))
    other = lax.ppermute(wgot, "core", SWAP)
    wk_par = jnp.where(core == 0, wgot, other)
    wv_par = jnp.where(core == 0, other, wgot)

    a_par, enc = attention_from(parts, pos, enc_gain, wk_par, wv_par, q_par)
    a_own = attention(enc, w_key, w_value, q_own)
    first, second, before = outputs(y, a_own, a_par, panel, False)

    def slow():
        enc = normed(half_rows(nbr_ids, embed, y), enc_gain)
        a_own = attention(enc, w_key, w_value, q_own)
        a_par = attention(enc, wk_par, wv_par, q_par)
        return finish(residual, *outputs(y, a_own, a_par, panel, True))

    return lax.cond(jnp.max(panel[:, width:, :].astype(jnp.float32)) > 0, slow, lambda: finish(residual, first, second, before))


def solution(mesh):
    fine = Mesh(mesh.devices.reshape(2, 4, 2, 8, 2), SEQ + MP)
    return jax.shard_map(
        per_device,
        mesh=fine,
        in_specs=(
            P(SEQ, MP),
            P(SEQ, MP),
            P(SEQ, None, None),
            P(MP, None),
            P(),
            P(None, MP),
            P(None, MP),
            P(MP + SEQ, None),
        ),
        out_specs=P(SEQ, MP),
        check_vma=False,
    )
```

```python
import functools

import jax
import jax.numpy as jnp
from jax import lax
from jax.experimental import pallas as pl
from jax.experimental.pallas import tpu as pltpu
from jax.sharding import Mesh
from jax.sharding import PartitionSpec as P

HD = 128
SPAN = 64
KEYS = 256
ROOM = 112
SEQ = ("yhi", "x", "core")
MP = ("z", "ylo")
SWAP = [(0, 1), (1, 0)]


def normed(rows, gain):
    wide = rows.astype(jnp.float32)
    power = jnp.mean(wide * wide, axis=-1, keepdims=True)
    return (wide * lax.rsqrt(power + 1e-06) * gain).astype(jnp.bfloat16)


def span_attention(enc, wk, wv, q, o):
    keys = jnp.dot(enc, wk[...], preferred_element_type=jnp.float32).astype(jnp.bfloat16)
    values = jnp.dot(enc, wv[...], preferred_element_type=jnp.float32).astype(jnp.bfloat16)
    places = [
        (slice(span * KEYS, (span + 1) * KEYS), slice(span * SPAN, (span + 1) * SPAN), slice(head * HD, (head + 1) * HD))
        for span in range(q.shape[0] // SPAN)
        for head in range(q.shape[1] // HD)
    ]
    scores = [
        lax.dot_general(q[t, d], keys[k, d], (((1,), (1,)), ((), ())), preferred_element_type=jnp.float32)
        * HD ** (-0.5)
        for k, t, d in places
    ]
    shifted = [jnp.exp(x - jnp.max(x, axis=-1, keepdims=True)) for x in scores]
    weights = [(x / jnp.sum(x, axis=-1, keepdims=True)).astype(jnp.bfloat16) for x in shifted]
    for (k, t, d), x in zip(places, weights):
        o[t, d] = jnp.dot(x, values[k, d], preferred_element_type=jnp.float32).astype(jnp.bfloat16)


def attend(enc_ref, wk, wv, q, o):
    span_attention(enc_ref[...], wk, wv, q, o)


def attention(enc, wk, wv, q):
    spans = enc.shape[0] // KEYS
    depth, width = wk.shape
    whole = pl.BlockSpec((depth, width), lambda i: (0, 0))
    tokens = pl.BlockSpec((2 * SPAN, width), lambda i: (i, 0))
    return pl.pallas_call(
        attend,
        grid=(spans // 2,),
        in_specs=[pl.BlockSpec((2 * KEYS, depth), lambda i: (i, 0)), whole, whole, tokens],
        out_specs=tokens,
        out_shape=jax.ShapeDtypeStruct((spans * SPAN, width), jnp.bfloat16),
        compiler_params=pltpu.CompilerParams(vmem_limit_bytes=24 * 2**20),
        cost_estimate=pl.CostEstimate(
            flops=spans * KEYS * depth * width * 4, bytes_accessed=6 * 2**20, transcendentals=spans * 2**16
        ),
    )(enc, wk, wv, q)


GROUPS = ((0, 3), (3, 5), (5, 7))
CHUNK = 256


def project(at_ref, *refs):
    panel, total, here, rows, block_sems, row_sems = refs[-6:]
    count = rows.shape[0]
    width = rows.shape[-1]
    whole, halves = refs[: count - 1], refs[count - 1 : -6]
    deep = rows.shape[2]
    copies = []
    for i in range(count):
        to = pl.ds(i * width, width)
        if i > 0:
            pieces = [pltpu.make_async_copy(whole[i - 1], here.at[:, to], block_sems.at[i])]
        else:
            half = halves[0].shape[0]
            pieces = [
                pltpu.make_async_copy(halves[0], here.at[pl.ds(0, half), to], block_sems.at[0]),
                pltpu.make_async_copy(halves[1], here.at[pl.ds(half, half), to], block_sems.at[count]),
            ]
        from_panel = pl.ds(pl.multiple_of(at_ref[i] * deep, deep), deep)
        copies.append((*pieces, pltpu.make_async_copy(panel.at[:, from_panel, :], rows.at[i], row_sems.at[i])))
    for those in copies:
        for copy in those:
            copy.start()
    for first, last in GROUPS:
        for those in copies[first:last]:
            for copy in those:
                copy.wait()
        attn = here[:, first * width : last * width]
        for side in range(2):
            for start in range(0, width, CHUNK):
                columns = slice(start, start + CHUNK)
                w = rows[first:last, :, side * (deep // 2) : (side + 1) * (deep // 2), columns]
                part = jnp.dot(attn, w.reshape(-1, CHUNK), preferred_element_type=jnp.float32)
                if first == 0:
                    total[side, :, columns] = part
                else:
                    total[side, :, columns] += part


def projected(at, blocks, panel):
    count = len(blocks) - 1
    tokens, width = blocks[0].shape
    seqs = panel.shape[0]
    anywhere = pl.BlockSpec(memory_space=pl.ANY)
    return pl.pallas_call(
        project,
        in_specs=[pl.BlockSpec(memory_space=pltpu.SMEM)] + [anywhere] * (count + 2),
        out_specs=pl.BlockSpec(memory_space=pltpu.VMEM),
        out_shape=jax.ShapeDtypeStruct((2, tokens, width), jnp.float32),
        scratch_shapes=[
            pltpu.VMEM((tokens, count * width), jnp.bfloat16),
            pltpu.VMEM((count, seqs, 2 * width // seqs, width), jnp.bfloat16),
            pltpu.SemaphoreType.DMA((count + 1,)),
            pltpu.SemaphoreType.DMA((count,)),
        ],
        compiler_params=pltpu.CompilerParams(vmem_limit_bytes=40 * 2**20),
        cost_estimate=pl.CostEstimate(
            flops=4 * count * tokens * width * width, bytes_accessed=16 * 2**20, transcendentals=0
        ),
    )(at, *blocks, panel)


def project_last(at_ref, near_ref, far_ref, panel_ref, sum_ref, own_ref, par_ref):
    half, width = near_ref.shape
    deep = panel_ref.shape[1] // 2
    for side, out in ((0, own_ref), (1, par_ref)):
        w = panel_ref[:, side * deep : (side + 1) * deep, :].reshape(width, width)
        for at, block in ((0, near_ref), (1, far_ref)):
            part = jnp.dot(block[...], w, preferred_element_type=jnp.float32)
            place = pl.ds(pl.multiple_of((at ^ at_ref[1]) * half, half), half)
            out[place, :] = (sum_ref[side, at * half : (at + 1) * half, :] + part).astype(out.dtype)


def projected_last(at, near, far, panel, sums):
    half, width = near.shape
    seqs = panel.shape[0]
    block = pl.BlockSpec((half, width), lambda i, at: (0, 0))
    whole = pl.BlockSpec((2 * half, width), lambda i, at: (0, 0))
    return pl.pallas_call(
        project_last,
        grid_spec=pltpu.PrefetchScalarGridSpec(
            num_scalar_prefetch=1,
            grid=(1,),
            in_specs=[
                block,
                block,
                pl.BlockSpec((seqs, 2 * width // seqs, width), lambda i, at: (0, at[0], 0)),
                pl.BlockSpec(sums.shape, lambda i, at: (0, 0, 0)),
            ],
            out_specs=[whole, whole],
        ),
        out_shape=[
            jax.ShapeDtypeStruct((2 * half, width), jnp.float32),
            jax.ShapeDtypeStruct((2 * half, width), jnp.bfloat16),
        ],
        compiler_params=pltpu.CompilerParams(vmem_limit_bytes=32 * 2**20),
        cost_estimate=pl.CostEstimate(flops=8 * half * width * width, bytes_accessed=4 * 2**20, transcendentals=0),
    )(at, near, far, panel, sums)


def half_rows(ids, embed, y):
    zs = lax.axis_size("z")
    block = embed.shape[0]
    each = ids.size // 2 // zs
    order = ids.reshape(2, zs, each).transpose(1, 0, 2).reshape(-1)
    local = order - lax.axis_index(MP) * block
    inside = jnp.logical_and(local >= 0, local < block)
    picked = jnp.take(embed, jnp.clip(local, 0, block - 1), axis=0, mode="clip")
    picked = jnp.where(inside[:, None], picked, jnp.zeros_like(picked))
    part = lax.psum_scatter(picked, "z", scatter_dimension=0, tiled=True).reshape(2, each, -1)
    kept = lax.dynamic_index_in_dim(part, y, 0, keepdims=False)
    sent = lax.dynamic_index_in_dim(part, 1 - y, 0, keepdims=False)
    rows = kept + lax.ppermute(sent, "ylo", SWAP)
    return lax.all_gather(rows, "z", axis=0, tiled=True)


def choose(where_ref, ids_ref, slots_ref, *, block):
    me, y = where_ref[0], where_ref[1]
    rows, lanes = ids_ref.shape
    local = ids_ref[...] - me * block
    mine = jnp.logical_and(local >= 0, local < block)
    hot = mine.astype(jnp.float32)
    upper = (
        lax.broadcasted_iota(jnp.int32, (lanes, lanes), 0) < lax.broadcasted_iota(jnp.int32, (lanes, lanes), 1)
    ).astype(jnp.bfloat16)
    before = jnp.dot(hot.astype(jnp.bfloat16), upper, preferred_element_type=jnp.float32)
    many = jnp.sum(hot, axis=1, keepdims=True)
    ranks = jnp.concatenate([before] * (lanes // rows), axis=0).T
    locals_ = jnp.concatenate([jnp.where(mine, local, -1).astype(jnp.float32)] * (lanes // rows), axis=0).T
    placef = lax.broadcasted_iota(jnp.int32, (lanes, lanes), 1).astype(jnp.float32)
    each = rows // 2
    for half in range(2):
        total = jnp.zeros((lanes, lanes), jnp.float32)
        seen = jnp.zeros((1, 1), jnp.float32)
        for row in range(half * each, half * each + each):
            column = locals_[:, row : row + 1]
            chosen = jnp.logical_and(ranks[:, row : row + 1] + seen == placef, column >= 0)
            total = total + jnp.where(chosen, column, 0.0)
            seen = seen + many[row : row + 1, :]
        slots = jnp.broadcast_to(jnp.sum(total, axis=0, keepdims=True), (8, lanes)).astype(jnp.int32)
        slots_ref[pl.ds(pl.multiple_of((half ^ y) * 8, 8), 8), :] = slots


def chosen_rows(ids, where, block):
    vmem = pl.BlockSpec(memory_space=pltpu.VMEM)
    return pl.pallas_call(
        functools.partial(choose, block=block),
        in_specs=[pl.BlockSpec(memory_space=pltpu.SMEM), vmem],
        out_specs=vmem,
        out_shape=jax.ShapeDtypeStruct((16, ids.shape[1]), jnp.int32),
        compiler_params=pltpu.CompilerParams(vmem_limit_bytes=8 * 2**20),
        cost_estimate=pl.CostEstimate(flops=2**24, bytes_accessed=2**14, transcendentals=0),
    )(where, ids)


def plan(where_ref, ids_ref, pos_ref, over_ref, *, block, room):
    y, z = where_ref[1], where_ref[2]
    rows, lanes = ids_ref.shape
    each = rows // 2
    lane = lax.broadcasted_iota(jnp.int32, (1, lanes), 1)
    base = (((z - (lane >> 1)) & 7) * (2 * room) + jnp.where((lane & 1) == y, 0, room)).astype(jnp.float32)
    lower = (
        lax.broadcasted_iota(jnp.int32, (lanes, lanes), 0) > lax.broadcasted_iota(jnp.int32, (lanes, lanes), 1)
    ).astype(jnp.bfloat16)
    place = lax.broadcasted_iota(jnp.int32, (lanes, lanes), 1)
    most = jnp.zeros((1, lanes), jnp.float32)
    for side in range(2):
        half = y if side == 0 else 1 - y
        owners = ids_ref[pl.ds(pl.multiple_of(half * each, each), each), :] // block
        columns = jnp.concatenate([owners.astype(jnp.float32)] * (lanes // each), axis=0).T
        seen = jnp.zeros((1, lanes), jnp.float32)
        for row in range(each):
            hot = (columns[:, row : row + 1].astype(jnp.int32) == place).astype(jnp.float32)
            if side == 0:
                before = jnp.dot(lower, hot.astype(jnp.bfloat16), preferred_element_type=jnp.float32) + seen
                pos = jnp.sum(hot * (before + base), axis=1, keepdims=True)
                pos_ref[row * lanes : (row + 1) * lanes, :] = jnp.broadcast_to(pos, (lanes, lanes)).astype(jnp.int32)
            seen = seen + jnp.sum(hot, axis=0, keepdims=True)
        most = jnp.maximum(most, seen)
    over = jnp.max((most > room).astype(jnp.float32), axis=1, keepdims=True)
    over_ref[...] = jnp.broadcast_to(over, over_ref.shape).astype(over_ref.dtype)


def planned(ids, where, block, room, width):
    lanes = ids.shape[1]
    vmem = pl.BlockSpec(memory_space=pltpu.VMEM)
    return pl.pallas_call(
        functools.partial(plan, block=block, room=room),
        in_specs=[pl.BlockSpec(memory_space=pltpu.SMEM), vmem],
        out_specs=[vmem, vmem],
        out_shape=[
            jax.ShapeDtypeStruct((ids.size // 2, lanes), jnp.int32),
            jax.ShapeDtypeStruct((16, width), jnp.bfloat16),
        ],
        compiler_params=pltpu.CompilerParams(vmem_limit_bytes=16 * 2**20),
        cost_estimate=pl.CostEstimate(flops=2**27, bytes_accessed=2**20, transcendentals=0),
    )(where, ids)


def attend_from(tables, *refs):
    parts = refs[:tables]
    pos_ref, gain_ref, wk, wv, q, o, enc_ref, table, sems = refs[tables:]

    @pl.when(pl.program_id(0) == 0)
    def _():
        copies, start = [], 0
        for i, part in enumerate(parts):
            copies.append(pltpu.make_async_copy(part, table.at[pl.ds(start, part.shape[0]), :], sems.at[i]))
            start += part.shape[0]
        for copy in copies:
            copy.start()
        for copy in copies:
            copy.wait()

    pos = pos_ref[...]
    lanes = pos.shape[1]
    lane = lax.broadcasted_iota(jnp.int32, pos.shape, 1)
    hot = jnp.concatenate(
        [(pos == lane + k * lanes).astype(jnp.bfloat16) for k in range(table.shape[0] // lanes)], axis=1
    )
    enc = normed(jnp.dot(hot, table[...], preferred_element_type=jnp.float32), gain_ref[...])
    enc_ref[...] = enc
    span_attention(enc, wk, wv, q, o)


def attention_from(parts, pos, gain, wk, wv, q):
    spans = pos.shape[0] // KEYS
    depth = parts[0].shape[1]
    width = wk.shape[1]
    whole = pl.BlockSpec((depth, width), lambda i: (0, 0))
    tokens = pl.BlockSpec((2 * SPAN, width), lambda i: (i, 0))
    span = pl.BlockSpec((2 * KEYS, depth), lambda i: (i, 0))
    return pl.pallas_call(
        functools.partial(attend_from, len(parts)),
        grid=(spans // 2,),
        in_specs=[pl.BlockSpec(memory_space=pl.ANY)] * len(parts)
        + [
            pl.BlockSpec((2 * KEYS, pos.shape[1]), lambda i: (i, 0)),
            pl.BlockSpec((1, depth), lambda i: (0, 0)),
            whole, whole, tokens,
        ],
        out_specs=[tokens, span],
        out_shape=[
            jax.ShapeDtypeStruct((spans * SPAN, width), jnp.bfloat16),
            jax.ShapeDtypeStruct((spans * KEYS, depth), jnp.bfloat16),
        ],
        scratch_shapes=[
            pltpu.VMEM((sum(part.shape[0] for part in parts), depth), jnp.bfloat16),
            pltpu.SemaphoreType.DMA((len(parts),)),
        ],
        compiler_params=pltpu.CompilerParams(vmem_limit_bytes=48 * 2**20),
        cost_estimate=pl.CostEstimate(
            flops=spans * KEYS * depth * width * 8, bytes_accessed=12 * 2**20, transcendentals=spans * 2**17
        ),
    )(*parts, pos, gain.reshape(1, -1), wk, wv, q)


def regroup(y_ref, w_ref, out_ref):
    pieces, sides, _, width = out_ref.shape
    for piece in range(pieces):
        for side in range(sides):
            start = pl.multiple_of((piece * sides + (side ^ y_ref[0])) * width, width)
            out_ref[piece, side] = w_ref[:, pl.ds(start, width)]


def regrouped(y, w, pieces, width):
    vmem = pl.BlockSpec(memory_space=pltpu.VMEM)
    return pl.pallas_call(
        regroup,
        in_specs=[pl.BlockSpec(memory_space=pltpu.SMEM), vmem],
        out_specs=vmem,
        out_shape=jax.ShapeDtypeStruct((pieces, 2, w.shape[0], width), w.dtype),
        compiler_params=pltpu.CompilerParams(vmem_limit_bytes=8 * 2**20),
        cost_estimate=pl.CostEstimate(flops=0, bytes_accessed=2 * w.size * 2, transcendentals=0),
    )(y.reshape(1), w)


def gather_z(x):
    n = lax.axis_size("z")
    blocks = lax.all_gather(x, "z")
    z = lax.axis_index("z")
    return [lax.dynamic_index_in_dim(blocks, lax.rem(z + n - d, n), 0, keepdims=False) for d in range(n)]


def hop(x, axis, by):
    n = lax.axis_size(axis)
    return lax.ppermute(x, axis, [(i, (i + by) % n) for i in range(n)])


def both_ways(right, left):
    return hop(right, "z", 1), hop(left, "z", -1)


def first_step(near, far):
    return tuple(jnp.concatenate(pair, axis=0) for pair in zip(both_ways(near, near), both_ways(far, far)))


def last_step(*steps):
    right, left = zip(*steps)
    half = right[-1].shape[0] // 2
    return [*right, hop(right[-1][:half], "z", 1), hop(left[-1][half:], "z", -1), *left[::-1]]


def outputs(y, near, far, blocks, panel):
    z, zs, seqs = lax.axis_index("z"), lax.axis_size("z"), lax.axis_size(SEQ)
    order = (0, 1, zs - 1, 2, zs - 2, 3, zs - 3)
    at = jnp.stack([lax.rem(z + zs - d, zs) for d in order])
    sums = projected(at, [*(blocks[d - 1 if d < zs // 2 else d] for d in order[1:]), near, far], panel)
    at = jnp.stack([lax.rem(z + zs // 2, zs), y])
    own, par = projected_last(at, blocks[zs // 2 - 1], blocks[zs // 2], panel, sums)
    end = slice(own.shape[0] - SPAN, None)
    onward = [(2 * i + side, 2 * i + 2 + side) for i in range(seqs - 1) for side in range(2)]
    across = [(2 * i + side, 2 * i + 3 - side) for i in range(seqs - 1) for side in range(2)]
    other = lax.ppermute(par, "ylo", SWAP)
    before = lax.ppermute(own[end], SEQ + ("ylo",), onward)
    before += lax.ppermute(par[end], SEQ + ("ylo",), across).astype(jnp.float32)
    return own, other, before


def finish(residual, own, other, before):
    shifted = own + other.astype(jnp.float32)
    return residual + jnp.concatenate([before[1:], shifted[: own.shape[0] - SPAN + 1]], axis=0)


def per_device(query, residual, nbr_ids, embed, enc_gain, w_key, w_value, w_out):
    tokens, width = query.shape
    half = tokens // 2
    y = lax.axis_index("ylo")
    z = lax.axis_index("z")
    core = lax.axis_index("core")
    zs = lax.axis_size("z")
    seqs = lax.axis_size(SEQ)

    mine = lax.all_to_all(regrouped(y, w_out, zs, width), "z", 0, 0, tiled=True)

    where = jnp.stack([lax.axis_index(MP), y, z]).astype(jnp.int32)
    ids = nbr_ids.reshape(-1, nbr_ids.shape[-1])
    slots = chosen_rows(ids, where, embed.shape[0])
    chosen = jnp.concatenate([slots[0, :ROOM], slots[8, :ROOM]])
    picked = embed.at[chosen].get(mode="promise_in_bounds")

    wgot = lax.ppermute(jnp.where(core == 0, w_key, w_value), "ylo", SWAP)
    picked_far, wgot = lax.optimization_barrier((picked[ROOM:], wgot))
    got = lax.ppermute(picked_far, "ylo", SWAP)

    step1 = first_step(picked[:ROOM], got)

    ids, query, _ = lax.optimization_barrier((ids, query, got))
    pos, over = planned(ids, where, embed.shape[0], ROOM, width)
    mine = jnp.concatenate([mine.reshape(-1, width), over], axis=0)
    mine, _ = lax.optimization_barrier((mine, step1))
    panel = lax.all_gather(mine, SEQ, axis=0, tiled=False)

    following = lax.ppermute(query[:SPAN], SEQ, [(i + 1, i) for i in range(seqs - 1)])
    moved = jnp.concatenate([query[SPAN - 1 :], following[: SPAN - 1]], axis=0).reshape(2, half, width)
    step1, moved = lax.optimization_barrier((step1, moved))
    step2 = both_ways(*step1)
    q_own = lax.dynamic_index_in_dim(moved, y, 0, keepdims=False)
    q_sent = lax.dynamic_index_in_dim(moved, 1 - y, 0, keepdims=False)
    wgot, step1 = lax.optimization_barrier((wgot, step1))
    other = lax.ppermute(wgot, "core", SWAP)
    wk_par = jnp.where(core == 0, wgot, other)
    wv_par = jnp.where(core == 0, other, wgot)
    step2, q_own, q_sent, wk_par, wv_par = lax.optimization_barrier((step2, q_own, q_sent, wk_par, wv_par))
    step3 = both_ways(*step2)
    q_par = lax.ppermute(q_sent, "ylo", SWAP)

    parts = [picked[:ROOM], got, *last_step(step1, step2, step3)]
    a_par, enc = attention_from(parts, pos, enc_gain, wk_par, wv_par, q_par)
    a_rest = lax.ppermute(a_par, "ylo", SWAP)
    a_own = attention(enc, w_key, w_value, q_own)
    step1 = first_step(a_own, a_rest)
    step2 = both_ways(*step1)
    step3 = both_ways(*step2)
    fast = outputs(y, a_own, a_rest, last_step(step1, step2, step3), panel)

    def slow():
        enc = normed(half_rows(nbr_ids, embed, y), enc_gain)
        a_rest = lax.ppermute(attention(enc, wk_par, wv_par, q_par), "ylo", SWAP)
        a_own = attention(enc, w_key, w_value, q_own)
        blocks = gather_z(jnp.concatenate([a_own, a_rest], axis=0))
        across = blocks[zs // 2]
        blocks = [*blocks[1 : zs // 2], across[:half], across[half:], *blocks[zs // 2 + 1 :]]
        return finish(residual, *outputs(y, a_own, a_rest, blocks, panel))

    over = jnp.max(panel[:, width:, :]).astype(jnp.float32) > 0
    return lax.cond(over, slow, lambda: finish(residual, *fast))


def solution(mesh):
    fine = Mesh(mesh.devices.reshape(2, 4, 2, 8, 2), SEQ + MP)
    return jax.shard_map(
        per_device,
        mesh=fine,
        in_specs=(
            P(SEQ, MP),
            P(SEQ, MP),
            P(SEQ, None, None),
            P(MP, None),
            P(),
            P(None, MP),
            P(None, MP),
            P(MP + SEQ, None),
        ),
        out_specs=P(SEQ, MP),
        check_vma=False,
    )
```

```python
import functools

import jax
import jax.numpy as jnp
from jax import lax
from jax.experimental import pallas as pl
from jax.experimental.pallas import tpu as pltpu
from jax.sharding import Mesh
from jax.sharding import PartitionSpec as P

HD = 128
LANES = 128
SPAN = 64
KEYS = 256
ROOM = 112
SEQ = ("yhi", "x", "core")
MP = ("z", "ylo")
SWAP = [(0, 1), (1, 0)]


def normed(rows, gain):
    wide = rows.astype(jnp.float32)
    power = jnp.mean(wide * wide, axis=-1, keepdims=True)
    return (wide * lax.rsqrt(power + 1e-06) * gain).astype(jnp.bfloat16)


def span_attention(enc, wk, wv, q, o):
    keys = jnp.dot(enc, wk[...], preferred_element_type=jnp.float32).astype(jnp.bfloat16)
    values = jnp.dot(enc, wv[...], preferred_element_type=jnp.float32).astype(jnp.bfloat16)
    places = [
        (slice(span * KEYS, (span + 1) * KEYS), slice(span * SPAN, (span + 1) * SPAN), slice(head * HD, (head + 1) * HD))
        for span in range(q.shape[0] // SPAN)
        for head in range(q.shape[1] // HD)
    ]
    scores = [
        lax.dot_general(q[t, d], keys[k, d], (((1,), (1,)), ((), ())), preferred_element_type=jnp.float32)
        * HD ** (-0.5)
        for k, t, d in places
    ]
    shifted = [jnp.exp(x - jnp.max(x, axis=-1, keepdims=True)) for x in scores]
    weights = [(x / jnp.sum(x, axis=-1, keepdims=True)).astype(jnp.bfloat16) for x in shifted]
    for (k, t, d), x in zip(places, weights):
        o[t, d] = jnp.dot(x, values[k, d], preferred_element_type=jnp.float32).astype(jnp.bfloat16)


def attend(enc_ref, wk, wv, q, o):
    span_attention(enc_ref[...], wk, wv, q, o)


def attention(enc, wk, wv, q):
    spans = enc.shape[0] // KEYS
    depth, width = wk.shape
    whole = pl.BlockSpec((depth, width), lambda i: (0, 0))
    tokens = pl.BlockSpec((2 * SPAN, width), lambda i: (i, 0))
    return pl.pallas_call(
        attend,
        grid=(spans // 2,),
        in_specs=[pl.BlockSpec((2 * KEYS, depth), lambda i: (i, 0)), whole, whole, tokens],
        out_specs=tokens,
        out_shape=jax.ShapeDtypeStruct((spans * SPAN, width), jnp.bfloat16),
        compiler_params=pltpu.CompilerParams(vmem_limit_bytes=24 * 2**20),
        cost_estimate=pl.CostEstimate(
            flops=spans * KEYS * depth * width * 4, bytes_accessed=6 * 2**20, transcendentals=spans * 2**16
        ),
    )(enc, wk, wv, q)


GROUPS = ((0, 3), (3, 5), (5, 7))
CHUNK = 256


def project(at_ref, *refs):
    ours, theirs, total, here, rows, block_sems, row_sems = refs[-7:]
    count = rows.shape[0]
    width = rows.shape[-1]
    whole, halves = refs[: count - 1], refs[count - 1 : -7]
    seqs, deep = rows.shape[1], rows.shape[2]
    level = at_ref[count]
    copies = []
    for i in range(count):
        to = pl.ds(i * width, width)
        if i > 0:
            pieces = [pltpu.make_async_copy(whole[i - 1], here.at[:, to], block_sems.at[i])]
        else:
            half = halves[0].shape[0]
            pieces = [
                pltpu.make_async_copy(halves[0], here.at[pl.ds(0, half), to], block_sems.at[0]),
                pltpu.make_async_copy(halves[1], here.at[pl.ds(half, half), to], block_sems.at[count]),
            ]
        from_panel = pl.ds(pl.multiple_of(at_ref[i] * deep, deep), deep)
        mine = pl.ds(pl.multiple_of(level * (seqs // 2), seqs // 2), seqs // 2)
        other = pl.ds(pl.multiple_of((1 - level) * (seqs // 2), seqs // 2), seqs // 2)
        copies.append(
            (
                *pieces,
                pltpu.make_async_copy(ours.at[:, from_panel, :], rows.at[i, mine], row_sems.at[i, 0]),
                pltpu.make_async_copy(theirs.at[:, from_panel, :], rows.at[i, other], row_sems.at[i, 1]),
            )
        )
    for three in copies:
        for copy in three:
            copy.start()
    for first, last in GROUPS:
        for three in copies[first:last]:
            for copy in three:
                copy.wait()
        attn = here[:, first * width : last * width]
        for side in range(2):
            for start in range(0, width, CHUNK):
                columns = slice(start, start + CHUNK)
                w = rows[first:last, :, side * (deep // 2) : (side + 1) * (deep // 2), columns]
                part = jnp.dot(attn, w.reshape(-1, CHUNK), preferred_element_type=jnp.float32)
                if first == 0:
                    total[side, :, columns] = part
                else:
                    total[side, :, columns] += part


def projected(at, blocks, ours, theirs):
    count = len(blocks) - 1
    tokens, width = blocks[0].shape
    seqs = 2 * ours.shape[0]
    anywhere = pl.BlockSpec(memory_space=pl.ANY)
    return pl.pallas_call(
        project,
        in_specs=[pl.BlockSpec(memory_space=pltpu.SMEM)] + [anywhere] * (count + 3),
        out_specs=pl.BlockSpec(memory_space=pltpu.VMEM),
        out_shape=jax.ShapeDtypeStruct((2, tokens, width), jnp.float32),
        scratch_shapes=[
            pltpu.VMEM((tokens, count * width), jnp.bfloat16),
            pltpu.VMEM((count, seqs, 2 * width // seqs, width), jnp.bfloat16),
            pltpu.SemaphoreType.DMA((count + 1,)),
            pltpu.SemaphoreType.DMA((count, 2)),
        ],
        compiler_params=pltpu.CompilerParams(vmem_limit_bytes=40 * 2**20),
        cost_estimate=pl.CostEstimate(
            flops=4 * count * tokens * width * width, bytes_accessed=16 * 2**20, transcendentals=0
        ),
    )(at, *blocks, ours, theirs)


def project_last(at_ref, near_ref, far_ref, ours_ref, theirs_ref, sum_ref, own_ref, par_ref):
    half, width = near_ref.shape
    deep = ours_ref.shape[1] // 2
    level = at_ref[2]
    for side, out in ((0, own_ref), (1, par_ref)):
        rows = slice(side * deep, (side + 1) * deep)
        for at, block in ((0, near_ref), (1, far_ref)):
            total = sum_ref[side, at * half : (at + 1) * half, :]
            for which, panel in ((level, ours_ref), (1 - level, theirs_ref)):
                columns = pl.ds(pl.multiple_of(which * (width // 2), width // 2), width // 2)
                w = panel[:, rows, :].reshape(width // 2, width)
                total = total + jnp.dot(block[:, columns], w, preferred_element_type=jnp.float32)
            place = pl.ds(pl.multiple_of((at ^ at_ref[1]) * half, half), half)
            out[place, :] = total.astype(out.dtype)


def projected_last(at, near, far, ours, theirs, sums):
    half, width = near.shape
    each = ours.shape[0]
    rows = width // each
    block = pl.BlockSpec((half, width), lambda i, at: (0, 0))
    whole = pl.BlockSpec((2 * half, width), lambda i, at: (0, 0))
    panel = pl.BlockSpec((each, rows, width), lambda i, at: (0, at[0], 0))
    return pl.pallas_call(
        project_last,
        grid_spec=pltpu.PrefetchScalarGridSpec(
            num_scalar_prefetch=1,
            grid=(1,),
            in_specs=[block, block, panel, panel, pl.BlockSpec(sums.shape, lambda i, at: (0, 0, 0))],
            out_specs=[whole, whole],
        ),
        out_shape=[
            jax.ShapeDtypeStruct((2 * half, width), jnp.float32),
            jax.ShapeDtypeStruct((2 * half, width), jnp.bfloat16),
        ],
        compiler_params=pltpu.CompilerParams(vmem_limit_bytes=32 * 2**20),
        cost_estimate=pl.CostEstimate(flops=8 * half * width * width, bytes_accessed=4 * 2**20, transcendentals=0),
    )(at, near, far, ours, theirs, sums)


def half_rows(ids, embed, y):
    zs = lax.axis_size("z")
    block = embed.shape[0]
    each = ids.size // 2 // zs
    order = ids.reshape(2, zs, each).transpose(1, 0, 2).reshape(-1)
    local = order - lax.axis_index(MP) * block
    inside = jnp.logical_and(local >= 0, local < block)
    picked = jnp.take(embed, jnp.clip(local, 0, block - 1), axis=0, mode="clip")
    picked = jnp.where(inside[:, None], picked, jnp.zeros_like(picked))
    part = lax.psum_scatter(picked, "z", scatter_dimension=0, tiled=True).reshape(2, each, -1)
    kept = lax.dynamic_index_in_dim(part, y, 0, keepdims=False)
    sent = lax.dynamic_index_in_dim(part, 1 - y, 0, keepdims=False)
    rows = kept + lax.ppermute(sent, "ylo", SWAP)
    return lax.all_gather(rows, "z", axis=0, tiled=True)


def choose(where_ref, ids_ref, slots_ref, *, block):
    me, y = where_ref[0], where_ref[1]
    rows, lanes = ids_ref.shape
    local = ids_ref[...] - me * block
    mine = jnp.logical_and(local >= 0, local < block)
    hot = mine.astype(jnp.float32)
    upper = (
        lax.broadcasted_iota(jnp.int32, (lanes, lanes), 0) < lax.broadcasted_iota(jnp.int32, (lanes, lanes), 1)
    ).astype(jnp.bfloat16)
    before = jnp.dot(hot.astype(jnp.bfloat16), upper, preferred_element_type=jnp.float32)
    many = jnp.sum(hot, axis=1, keepdims=True)
    ranks = jnp.concatenate([before] * (lanes // rows), axis=0).T
    locals_ = jnp.concatenate([jnp.where(mine, local, -1).astype(jnp.float32)] * (lanes // rows), axis=0).T
    placef = lax.broadcasted_iota(jnp.int32, (lanes, lanes), 1).astype(jnp.float32)
    each = rows // 2
    for half in range(2):
        total = jnp.zeros((lanes, lanes), jnp.float32)
        seen = jnp.zeros((1, 1), jnp.float32)
        for row in range(half * each, half * each + each):
            column = locals_[:, row : row + 1]
            chosen = jnp.logical_and(ranks[:, row : row + 1] + seen == placef, column >= 0)
            total = total + jnp.where(chosen, column, 0.0)
            seen = seen + many[row : row + 1, :]
        slots = jnp.broadcast_to(jnp.sum(total, axis=0, keepdims=True), (8, lanes)).astype(jnp.int32)
        slots_ref[pl.ds(pl.multiple_of((half ^ y) * 8, 8), 8), :] = slots


def chosen_rows(ids, where, block):
    vmem = pl.BlockSpec(memory_space=pltpu.VMEM)
    return pl.pallas_call(
        functools.partial(choose, block=block),
        in_specs=[pl.BlockSpec(memory_space=pltpu.SMEM), vmem],
        out_specs=vmem,
        out_shape=jax.ShapeDtypeStruct((16, ids.shape[1]), jnp.int32),
        compiler_params=pltpu.CompilerParams(vmem_limit_bytes=8 * 2**20),
        cost_estimate=pl.CostEstimate(flops=2**24, bytes_accessed=2**14, transcendentals=0),
    )(where, ids)


def late_place(room):
    return -(-14 * room // LANES) * LANES


def plan(where_ref, ids_ref, pos_ref, over_ref, *, block, room):
    y, z = where_ref[1], where_ref[2]
    rows, lanes = ids_ref.shape
    each = rows // 2
    lane = lax.broadcasted_iota(jnp.int32, (1, lanes), 1)
    steps = (z - (lane >> 1)) & 7
    block_at = jnp.where(steps == 4, late_place(room), jnp.where(steps < 4, steps, steps - 1) * (2 * room))
    base = (block_at + jnp.where((lane & 1) == y, 0, room)).astype(jnp.float32)
    lower = (
        lax.broadcasted_iota(jnp.int32, (lanes, lanes), 0) > lax.broadcasted_iota(jnp.int32, (lanes, lanes), 1)
    ).astype(jnp.bfloat16)
    place = lax.broadcasted_iota(jnp.int32, (lanes, lanes), 1)
    most = jnp.zeros((1, lanes), jnp.float32)
    for side in range(2):
        half = y if side == 0 else 1 - y
        owners = ids_ref[pl.ds(pl.multiple_of(half * each, each), each), :] // block
        columns = jnp.concatenate([owners.astype(jnp.float32)] * (lanes // each), axis=0).T
        seen = jnp.zeros((1, lanes), jnp.float32)
        for row in range(each):
            hot = (columns[:, row : row + 1].astype(jnp.int32) == place).astype(jnp.float32)
            if side == 0:
                before = jnp.dot(lower, hot.astype(jnp.bfloat16), preferred_element_type=jnp.float32) + seen
                pos = jnp.sum(hot * (before + base), axis=1, keepdims=True)
                pos_ref[row * lanes : (row + 1) * lanes, :] = jnp.broadcast_to(pos, (lanes, lanes)).astype(jnp.int32)
            seen = seen + jnp.sum(hot, axis=0, keepdims=True)
        most = jnp.maximum(most, seen)
    over = jnp.max((most > room).astype(jnp.float32), axis=1, keepdims=True)
    over_ref[...] = jnp.broadcast_to(over, over_ref.shape).astype(over_ref.dtype)


def planned(ids, where, block, room, width):
    lanes = ids.shape[1]
    vmem = pl.BlockSpec(memory_space=pltpu.VMEM)
    return pl.pallas_call(
        functools.partial(plan, block=block, room=room),
        in_specs=[pl.BlockSpec(memory_space=pltpu.SMEM), vmem],
        out_specs=[vmem, vmem],
        out_shape=[
            jax.ShapeDtypeStruct((ids.size // 2, lanes), jnp.int32),
            jax.ShapeDtypeStruct((16, width), jnp.bfloat16),
        ],
        compiler_params=pltpu.CompilerParams(vmem_limit_bytes=16 * 2**20),
        cost_estimate=pl.CostEstimate(flops=2**27, bytes_accessed=2**20, transcendentals=0),
    )(where, ids)


def spread(*refs):
    parts = refs[:-4]
    pos_ref, rows_ref, table, sems = refs[-4:]

    @pl.when(pl.program_id(0) == 0)
    def _():
        copies = []
        end = sum(part.shape[0] for part in parts)
        table[end:, :] = jnp.zeros_like(table[end:, :])
        for i, (part, start) in enumerate(zip(parts, places_of(parts))):
            copies.append(pltpu.make_async_copy(part, table.at[pl.ds(start, part.shape[0]), :], sems.at[i]))
        for copy in copies:
            copy.start()
        for copy in copies:
            copy.wait()

    rows_ref[...] = looked_up(pos_ref[...], table[...]).astype(jnp.bfloat16)


def places_of(parts):
    return [sum(part.shape[0] for part in parts[:i]) for i in range(len(parts))]


def looked_up(pos, table):
    lane = lax.broadcasted_iota(jnp.int32, pos.shape, 1)
    lanes = pos.shape[1]
    hot = [(pos == lane + start).astype(jnp.bfloat16) for start in range(0, table.shape[0], lanes)]
    return jnp.dot(jnp.concatenate(hot, axis=1), table, preferred_element_type=jnp.float32)


def spread_rows(parts, pos):
    deep, depth = late_place(ROOM), parts[0].shape[1]
    rows, lanes = 2 * KEYS, pos.shape[1]
    return pl.pallas_call(
        spread,
        grid=(pos.shape[0] // rows,),
        in_specs=[pl.BlockSpec(memory_space=pl.ANY)] * len(parts) + [pl.BlockSpec((rows, lanes), lambda i: (i, 0))],
        out_specs=pl.BlockSpec((rows, depth), lambda i: (i, 0)),
        out_shape=jax.ShapeDtypeStruct((pos.shape[0], depth), jnp.bfloat16),
        scratch_shapes=[pltpu.VMEM((deep, depth), jnp.bfloat16), pltpu.SemaphoreType.DMA((len(parts),))],
        compiler_params=pltpu.CompilerParams(vmem_limit_bytes=32 * 2**20),
        cost_estimate=pl.CostEstimate(
            flops=2 * pos.shape[0] * deep * depth, bytes_accessed=8 * 2**20, transcendentals=0
        ),
    )(*parts, pos)


def attend_last(rows_ref, near_ref, far_ref, pos_ref, gain_ref, wk, wv, q, o, enc_ref, table, *, place):
    @pl.when(pl.program_id(0) == 0)
    def _():
        table[...] = jnp.zeros_like(table)
        room = near_ref.shape[0]
        table[:room, :] = near_ref[...]
        table[room : 2 * room, :] = far_ref[...]

    wide = rows_ref[...].astype(jnp.float32) + looked_up(pos_ref[...] - place, table[...])
    enc = normed(wide, gain_ref[...])
    enc_ref[...] = enc
    span_attention(enc, wk, wv, q, o)


def attention_last(rows, near, far, pos, place, gain, wk, wv, q):
    spans = pos.shape[0] // KEYS
    room, depth = near.shape
    width = wk.shape[1]
    whole = pl.BlockSpec((depth, width), lambda i: (0, 0))
    part = pl.BlockSpec((room, depth), lambda i: (0, 0))
    tokens = pl.BlockSpec((2 * SPAN, width), lambda i: (i, 0))
    span = pl.BlockSpec((2 * KEYS, depth), lambda i: (i, 0))
    return pl.pallas_call(
        functools.partial(attend_last, place=place),
        grid=(spans // 2,),
        in_specs=[
            span,
            part,
            part,
            pl.BlockSpec((2 * KEYS, pos.shape[1]), lambda i: (i, 0)),
            pl.BlockSpec((1, depth), lambda i: (0, 0)),
            whole, whole, tokens,
        ],
        out_specs=[tokens, span],
        out_shape=[
            jax.ShapeDtypeStruct((spans * SPAN, width), jnp.bfloat16),
            jax.ShapeDtypeStruct((spans * KEYS, depth), jnp.bfloat16),
        ],
        scratch_shapes=[pltpu.VMEM((-(-2 * room // LANES) * LANES, depth), jnp.bfloat16)],
        compiler_params=pltpu.CompilerParams(vmem_limit_bytes=40 * 2**20),
        cost_estimate=pl.CostEstimate(
            flops=spans * KEYS * depth * width * 5, bytes_accessed=8 * 2**20, transcendentals=spans * 2**16
        ),
    )(rows, near, far, pos, gain.reshape(1, -1), wk, wv, q)


def regroup(y_ref, w_ref, out_ref):
    pieces, sides, _, width = out_ref.shape
    for piece in range(pieces):
        for side in range(sides):
            start = pl.multiple_of((piece * sides + (side ^ y_ref[0])) * width, width)
            out_ref[piece, side] = w_ref[:, pl.ds(start, width)]


def regrouped(y, w, pieces, width):
    vmem = pl.BlockSpec(memory_space=pltpu.VMEM)
    return pl.pallas_call(
        regroup,
        in_specs=[pl.BlockSpec(memory_space=pltpu.SMEM), vmem],
        out_specs=vmem,
        out_shape=jax.ShapeDtypeStruct((pieces, 2, w.shape[0], width), w.dtype),
        compiler_params=pltpu.CompilerParams(vmem_limit_bytes=8 * 2**20),
        cost_estimate=pl.CostEstimate(flops=0, bytes_accessed=2 * w.size * 2, transcendentals=0),
    )(y.reshape(1), w)


def gather_z(x):
    n = lax.axis_size("z")
    blocks = lax.all_gather(x, "z")
    z = lax.axis_index("z")
    return [lax.dynamic_index_in_dim(blocks, lax.rem(z + n - d, n), 0, keepdims=False) for d in range(n)]


def hop(x, axis, by):
    n = lax.axis_size(axis)
    return lax.ppermute(x, axis, [(i, (i + by) % n) for i in range(n)])


def both_ways(right, left):
    return hop(right, "z", 1), hop(left, "z", -1)


def first_step(near, far):
    return tuple(jnp.concatenate(pair, axis=0) for pair in zip(both_ways(near, near), both_ways(far, far)))


def last_step(*steps):
    right, left = zip(*steps)
    half = right[-1].shape[0] // 2
    return [*right, hop(right[-1][:half], "z", 1), hop(left[-1][half:], "z", -1), *left[::-1]]


def outputs(y, near, far, blocks, ours, theirs):
    z, zs, seqs = lax.axis_index("z"), lax.axis_size("z"), lax.axis_size(SEQ)
    order = (0, 1, zs - 1, 2, zs - 2, 3, zs - 3)
    level = lax.axis_index("yhi")
    at = jnp.stack([lax.rem(z + zs - d, zs) for d in order] + [level])
    sums = projected(at, [*(blocks[d - 1 if d < zs // 2 else d] for d in order[1:]), near, far], ours, theirs)
    at = jnp.stack([lax.rem(z + zs // 2, zs), y, level])
    own, par = projected_last(at, blocks[zs // 2 - 1], blocks[zs // 2], ours, theirs, sums)
    end = slice(own.shape[0] - SPAN, None)
    onward = [(2 * i + side, 2 * i + 2 + side) for i in range(seqs - 1) for side in range(2)]
    across = [(2 * i + side, 2 * i + 3 - side) for i in range(seqs - 1) for side in range(2)]
    other = lax.ppermute(par, "ylo", SWAP)
    before = lax.ppermute(own[end], SEQ + ("ylo",), onward)
    before += lax.ppermute(par[end], SEQ + ("ylo",), across).astype(jnp.float32)
    return own, other, before


def finish(residual, own, other, before):
    shifted = own + other.astype(jnp.float32)
    return residual + jnp.concatenate([before[1:], shifted[: own.shape[0] - SPAN + 1]], axis=0)


def per_device(query, residual, nbr_ids, embed, enc_gain, w_key, w_value, w_out):
    tokens, width = query.shape
    half = tokens // 2
    y = lax.axis_index("ylo")
    z = lax.axis_index("z")
    core = lax.axis_index("core")
    zs = lax.axis_size("z")
    seqs = lax.axis_size(SEQ)

    mine = lax.all_to_all(regrouped(y, w_out, zs, width), "z", 0, 0, tiled=True)

    where = jnp.stack([lax.axis_index(MP), y, z]).astype(jnp.int32)
    ids = nbr_ids.reshape(-1, nbr_ids.shape[-1])
    slots = chosen_rows(ids, where, embed.shape[0])
    chosen = jnp.concatenate([slots[0, :ROOM], slots[8, :ROOM]])
    picked = embed.at[chosen].get(mode="promise_in_bounds")

    wgot = lax.ppermute(jnp.where(core == 0, w_key, w_value), "ylo", SWAP)
    picked_far, wgot = lax.optimization_barrier((picked[ROOM:], wgot))
    got = lax.ppermute(picked_far, "ylo", SWAP)

    step1 = first_step(picked[:ROOM], got)

    ids, query, _ = lax.optimization_barrier((ids, query, got))
    pos, over = planned(ids, where, embed.shape[0], ROOM, width)
    mine = jnp.concatenate([mine.reshape(-1, width), over], axis=0)
    mine, _ = lax.optimization_barrier((mine, step1))
    ours = lax.all_gather(mine, SEQ[1:], axis=0, tiled=False)
    level = lax.ppermute(mine, "yhi", SWAP)

    following = lax.ppermute(query[:SPAN], SEQ, [(i + 1, i) for i in range(seqs - 1)])
    moved = jnp.concatenate([query[SPAN - 1 :], following[: SPAN - 1]], axis=0).reshape(2, half, width)
    step1, moved = lax.optimization_barrier((step1, moved))
    step2 = both_ways(*step1)
    q_own = lax.dynamic_index_in_dim(moved, y, 0, keepdims=False)
    q_sent = lax.dynamic_index_in_dim(moved, 1 - y, 0, keepdims=False)
    wgot, step1 = lax.optimization_barrier((wgot, step1))
    other = lax.ppermute(wgot, "core", SWAP)
    wk_par = jnp.where(core == 0, wgot, other)
    wv_par = jnp.where(core == 0, other, wgot)
    step2, q_own, q_sent, wk_par, wv_par, level = lax.optimization_barrier(
        (step2, q_own, q_sent, wk_par, wv_par, level)
    )
    theirs = lax.all_gather(level, SEQ[1:], axis=0, tiled=False)
    step3 = both_ways(*step2)
    q_par = lax.ppermute(q_sent, "ylo", SWAP)

    rights, lefts = zip(step1, step2, step3)
    rows = spread_rows([picked[:ROOM], got, *rights, *lefts[::-1]], pos)
    _, _, _, last_near, last_far, *_ = last_step(step1, step2, step3)
    a_par, enc = attention_last(rows, last_near, last_far, pos, late_place(ROOM), enc_gain, wk_par, wv_par, q_par)
    a_rest = lax.ppermute(a_par, "ylo", SWAP)
    a_own = attention(enc, w_key, w_value, q_own)
    step1 = first_step(a_own, a_rest)
    step2 = both_ways(*step1)
    step3 = both_ways(*step2)
    fast = outputs(y, a_own, a_rest, last_step(step1, step2, step3), ours, theirs)

    def slow():
        enc = normed(half_rows(nbr_ids, embed, y), enc_gain)
        a_rest = lax.ppermute(attention(enc, wk_par, wv_par, q_par), "ylo", SWAP)
        a_own = attention(enc, w_key, w_value, q_own)
        blocks = gather_z(jnp.concatenate([a_own, a_rest], axis=0))
        across = blocks[zs // 2]
        blocks = [*blocks[1 : zs // 2], across[:half], across[half:], *blocks[zs // 2 + 1 :]]
        return finish(residual, *outputs(y, a_own, a_rest, blocks, ours, theirs))

    over = jnp.maximum(jnp.max(ours[:, width:, :]), jnp.max(theirs[:, width:, :])).astype(jnp.float32) > 0
    return lax.cond(over, slow, lambda: finish(residual, *fast))


def solution(mesh):
    fine = Mesh(mesh.devices.reshape(2, 4, 2, 8, 2), SEQ + MP)
    return jax.shard_map(
        per_device,
        mesh=fine,
        in_specs=(
            P(SEQ, MP),
            P(SEQ, MP),
            P(SEQ, None, None),
            P(MP, None),
            P(),
            P(None, MP),
            P(None, MP),
            P(MP + SEQ, None),
        ),
        out_specs=P(SEQ, MP),
        check_vma=False,
    )
```

```python
import functools

import jax
import jax.numpy as jnp
from jax import lax
from jax.experimental import pallas as pl
from jax.experimental.pallas import tpu as pltpu
from jax.sharding import Mesh
from jax.sharding import PartitionSpec as P

HD = 128
LANES = 128
SPAN = 64
KEYS = 256
ROOM = 112
SEQ = ("yhi", "x", "core")
MP = ("z", "ylo")
SWAP = [(0, 1), (1, 0)]


def normed(rows, gain):
    wide = rows.astype(jnp.float32)
    power = jnp.mean(wide * wide, axis=-1, keepdims=True)
    return (wide * lax.rsqrt(power + 1e-06) * gain).astype(jnp.bfloat16)


def span_attention(enc, wk, wv, q, o):
    keys = jnp.dot(enc, wk[...], preferred_element_type=jnp.float32).astype(jnp.bfloat16)
    values = jnp.dot(enc, wv[...], preferred_element_type=jnp.float32).astype(jnp.bfloat16)
    places = [
        (slice(span * KEYS, (span + 1) * KEYS), slice(span * SPAN, (span + 1) * SPAN), slice(head * HD, (head + 1) * HD))
        for span in range(q.shape[0] // SPAN)
        for head in range(q.shape[1] // HD)
    ]
    scores = [
        lax.dot_general(q[t, d], keys[k, d], (((1,), (1,)), ((), ())), preferred_element_type=jnp.float32)
        * HD ** (-0.5)
        for k, t, d in places
    ]
    shifted = [jnp.exp(x - jnp.max(x, axis=-1, keepdims=True)) for x in scores]
    weights = [(x / jnp.sum(x, axis=-1, keepdims=True)).astype(jnp.bfloat16) for x in shifted]
    for (k, t, d), x in zip(places, weights):
        o[t, d] = jnp.dot(x, values[k, d], preferred_element_type=jnp.float32).astype(jnp.bfloat16)


def attend(enc_ref, wk, wv, q, o):
    span_attention(enc_ref[...], wk, wv, q, o)


def attention(enc, wk, wv, q):
    spans = enc.shape[0] // KEYS
    depth, width = wk.shape
    whole = pl.BlockSpec((depth, width), lambda i: (0, 0))
    tokens = pl.BlockSpec((2 * SPAN, width), lambda i: (i, 0))
    return pl.pallas_call(
        attend,
        grid=(spans // 2,),
        in_specs=[pl.BlockSpec((2 * KEYS, depth), lambda i: (i, 0)), whole, whole, tokens],
        out_specs=tokens,
        out_shape=jax.ShapeDtypeStruct((spans * SPAN, width), jnp.bfloat16),
        compiler_params=pltpu.CompilerParams(vmem_limit_bytes=24 * 2**20),
        cost_estimate=pl.CostEstimate(
            flops=spans * KEYS * depth * width * 4, bytes_accessed=6 * 2**20, transcendentals=spans * 2**16
        ),
    )(enc, wk, wv, q)


GROUPS = ((0, 3), (3, 5), (5, 7))
CHUNK = 256


def project(at_ref, *refs):
    ours, theirs, total, here, rows, block_sems, row_sems = refs[-7:]
    count = rows.shape[0]
    width = rows.shape[-1]
    whole, halves = refs[: count - 1], refs[count - 1 : -7]
    seqs, deep = rows.shape[1], rows.shape[2]
    level = at_ref[count]
    copies = []
    for i in range(count):
        to = pl.ds(i * width, width)
        if i > 0:
            pieces = [pltpu.make_async_copy(whole[i - 1], here.at[:, to], block_sems.at[i])]
        else:
            half = halves[0].shape[0]
            pieces = [
                pltpu.make_async_copy(halves[0], here.at[pl.ds(0, half), to], block_sems.at[0]),
                pltpu.make_async_copy(halves[1], here.at[pl.ds(half, half), to], block_sems.at[count]),
            ]
        from_panel = pl.ds(pl.multiple_of(at_ref[i] * deep, deep), deep)
        mine = pl.ds(pl.multiple_of(level * (seqs // 2), seqs // 2), seqs // 2)
        other = pl.ds(pl.multiple_of((1 - level) * (seqs // 2), seqs // 2), seqs // 2)
        copies.append(
            (
                *pieces,
                pltpu.make_async_copy(ours.at[:, from_panel, :], rows.at[i, mine], row_sems.at[i, 0]),
                pltpu.make_async_copy(theirs.at[:, from_panel, :], rows.at[i, other], row_sems.at[i, 1]),
            )
        )
    for three in copies:
        for copy in three:
            copy.start()
    for first, last in GROUPS:
        for three in copies[first:last]:
            for copy in three:
                copy.wait()
        attn = here[:, first * width : last * width]
        for side in range(2):
            for start in range(0, width, CHUNK):
                columns = slice(start, start + CHUNK)
                w = rows[first:last, :, side * (deep // 2) : (side + 1) * (deep // 2), columns]
                part = jnp.dot(attn, w.reshape(-1, CHUNK), preferred_element_type=jnp.float32)
                if first == 0:
                    total[side, :, columns] = part
                else:
                    total[side, :, columns] += part


def projected(at, blocks, ours, theirs):
    count = len(blocks) - 1
    tokens, width = blocks[0].shape
    seqs = 2 * ours.shape[0]
    anywhere = pl.BlockSpec(memory_space=pl.ANY)
    return pl.pallas_call(
        project,
        in_specs=[pl.BlockSpec(memory_space=pltpu.SMEM)] + [anywhere] * (count + 3),
        out_specs=pl.BlockSpec(memory_space=pltpu.VMEM),
        out_shape=jax.ShapeDtypeStruct((2, tokens, width), jnp.float32),
        scratch_shapes=[
            pltpu.VMEM((tokens, count * width), jnp.bfloat16),
            pltpu.VMEM((count, seqs, 2 * width // seqs, width), jnp.bfloat16),
            pltpu.SemaphoreType.DMA((count + 1,)),
            pltpu.SemaphoreType.DMA((count, 2)),
        ],
        compiler_params=pltpu.CompilerParams(vmem_limit_bytes=40 * 2**20),
        cost_estimate=pl.CostEstimate(
            flops=4 * count * tokens * width * width, bytes_accessed=16 * 2**20, transcendentals=0
        ),
    )(at, *blocks, ours, theirs)


def project_last(at_ref, near_ref, far_ref, ours_ref, theirs_ref, sum_ref, own_ref, par_ref):
    half, width = near_ref.shape
    deep = ours_ref.shape[1] // 2
    level = at_ref[2]
    for side, out in ((0, own_ref), (1, par_ref)):
        rows = slice(side * deep, (side + 1) * deep)
        for at, block in ((0, near_ref), (1, far_ref)):
            total = sum_ref[side, at * half : (at + 1) * half, :]
            for which, panel in ((level, ours_ref), (1 - level, theirs_ref)):
                columns = pl.ds(pl.multiple_of(which * (width // 2), width // 2), width // 2)
                w = panel[:, rows, :].reshape(width // 2, width)
                total = total + jnp.dot(block[:, columns], w, preferred_element_type=jnp.float32)
            place = pl.ds(pl.multiple_of((at ^ at_ref[1]) * half, half), half)
            out[place, :] = total.astype(out.dtype)


def projected_last(at, near, far, ours, theirs, sums):
    half, width = near.shape
    each = ours.shape[0]
    rows = width // each
    block = pl.BlockSpec((half, width), lambda i, at: (0, 0))
    whole = pl.BlockSpec((2 * half, width), lambda i, at: (0, 0))
    panel = pl.BlockSpec((each, rows, width), lambda i, at: (0, at[0], 0))
    return pl.pallas_call(
        project_last,
        grid_spec=pltpu.PrefetchScalarGridSpec(
            num_scalar_prefetch=1,
            grid=(1,),
            in_specs=[block, block, panel, panel, pl.BlockSpec(sums.shape, lambda i, at: (0, 0, 0))],
            out_specs=[whole, whole],
        ),
        out_shape=[
            jax.ShapeDtypeStruct((2 * half, width), jnp.float32),
            jax.ShapeDtypeStruct((2 * half, width), jnp.bfloat16),
        ],
        compiler_params=pltpu.CompilerParams(vmem_limit_bytes=32 * 2**20),
        cost_estimate=pl.CostEstimate(flops=8 * half * width * width, bytes_accessed=4 * 2**20, transcendentals=0),
    )(at, near, far, ours, theirs, sums)


def half_rows(ids, embed, y):
    zs = lax.axis_size("z")
    block = embed.shape[0]
    each = ids.size // 2 // zs
    order = ids.reshape(2, zs, each).transpose(1, 0, 2).reshape(-1)
    local = order - lax.axis_index(MP) * block
    inside = jnp.logical_and(local >= 0, local < block)
    picked = jnp.take(embed, jnp.clip(local, 0, block - 1), axis=0, mode="clip")
    picked = jnp.where(inside[:, None], picked, jnp.zeros_like(picked))
    part = lax.psum_scatter(picked, "z", scatter_dimension=0, tiled=True).reshape(2, each, -1)
    kept = lax.dynamic_index_in_dim(part, y, 0, keepdims=False)
    sent = lax.dynamic_index_in_dim(part, 1 - y, 0, keepdims=False)
    rows = kept + lax.ppermute(sent, "ylo", SWAP)
    return lax.all_gather(rows, "z", axis=0, tiled=True)


def choose(where_ref, ids_ref, slots_ref, *, block):
    me, y = where_ref[0], where_ref[1]
    rows, lanes = ids_ref.shape
    local = ids_ref[...] - me * block
    mine = jnp.logical_and(local >= 0, local < block)
    hot = mine.astype(jnp.float32)
    upper = (
        lax.broadcasted_iota(jnp.int32, (lanes, lanes), 0) < lax.broadcasted_iota(jnp.int32, (lanes, lanes), 1)
    ).astype(jnp.bfloat16)
    before = jnp.dot(hot.astype(jnp.bfloat16), upper, preferred_element_type=jnp.float32)
    many = jnp.sum(hot, axis=1, keepdims=True)
    ranks = jnp.concatenate([before] * (lanes // rows), axis=0).T
    locals_ = jnp.concatenate([jnp.where(mine, local, -1).astype(jnp.float32)] * (lanes // rows), axis=0).T
    placef = lax.broadcasted_iota(jnp.int32, (lanes, lanes), 1).astype(jnp.float32)
    each = rows // 2
    for half in range(2):
        total = jnp.zeros((lanes, lanes), jnp.float32)
        seen = jnp.zeros((1, 1), jnp.float32)
        for row in range(half * each, half * each + each):
            column = locals_[:, row : row + 1]
            chosen = jnp.logical_and(ranks[:, row : row + 1] + seen == placef, column >= 0)
            total = total + jnp.where(chosen, column, 0.0)
            seen = seen + many[row : row + 1, :]
        slots = jnp.broadcast_to(jnp.sum(total, axis=0, keepdims=True), (8, lanes)).astype(jnp.int32)
        slots_ref[pl.ds(pl.multiple_of((half ^ y) * 8, 8), 8), :] = slots


def chosen_rows(ids, where, block):
    vmem = pl.BlockSpec(memory_space=pltpu.VMEM)
    return pl.pallas_call(
        functools.partial(choose, block=block),
        in_specs=[pl.BlockSpec(memory_space=pltpu.SMEM), vmem],
        out_specs=vmem,
        out_shape=jax.ShapeDtypeStruct((16, ids.shape[1]), jnp.int32),
        compiler_params=pltpu.CompilerParams(vmem_limit_bytes=8 * 2**20),
        cost_estimate=pl.CostEstimate(flops=2**24, bytes_accessed=2**14, transcendentals=0),
    )(where, ids)


def late_place(room):
    return -(-14 * room // LANES) * LANES


def plan(where_ref, ids_ref, pos_ref, over_ref, *, block, room):
    y, z = where_ref[1], where_ref[2]
    rows, lanes = ids_ref.shape
    each = rows // 2
    lane = lax.broadcasted_iota(jnp.int32, (1, lanes), 1)
    steps = (z - (lane >> 1)) & 7
    block_at = jnp.where(steps == 4, late_place(room), jnp.where(steps < 4, steps, steps - 1) * (2 * room))
    base = (block_at + jnp.where((lane & 1) == y, 0, room)).astype(jnp.float32)
    lower = (
        lax.broadcasted_iota(jnp.int32, (lanes, lanes), 0) > lax.broadcasted_iota(jnp.int32, (lanes, lanes), 1)
    ).astype(jnp.bfloat16)
    place = lax.broadcasted_iota(jnp.int32, (lanes, lanes), 1)
    most = jnp.zeros((1, lanes), jnp.float32)
    for side in range(2):
        half = y if side == 0 else 1 - y
        owners = ids_ref[pl.ds(pl.multiple_of(half * each, each), each), :] // block
        columns = jnp.concatenate([owners.astype(jnp.float32)] * (lanes // each), axis=0).T
        seen = jnp.zeros((1, lanes), jnp.float32)
        for row in range(each):
            hot = (columns[:, row : row + 1].astype(jnp.int32) == place).astype(jnp.float32)
            if side == 0:
                before = jnp.dot(lower, hot.astype(jnp.bfloat16), preferred_element_type=jnp.float32) + seen
                pos = jnp.sum(hot * (before + base), axis=1, keepdims=True)
                pos_ref[row * lanes : (row + 1) * lanes, :] = jnp.broadcast_to(pos, (lanes, lanes)).astype(jnp.int32)
            seen = seen + jnp.sum(hot, axis=0, keepdims=True)
        most = jnp.maximum(most, seen)
    over = jnp.max((most > room).astype(jnp.float32), axis=1, keepdims=True)
    over_ref[...] = jnp.broadcast_to(over, over_ref.shape).astype(over_ref.dtype)


def planned(ids, where, block, room, width):
    lanes = ids.shape[1]
    vmem = pl.BlockSpec(memory_space=pltpu.VMEM)
    return pl.pallas_call(
        functools.partial(plan, block=block, room=room),
        in_specs=[pl.BlockSpec(memory_space=pltpu.SMEM), vmem],
        out_specs=[vmem, vmem],
        out_shape=[
            jax.ShapeDtypeStruct((ids.size // 2, lanes), jnp.int32),
            jax.ShapeDtypeStruct((16, width), jnp.bfloat16),
        ],
        compiler_params=pltpu.CompilerParams(vmem_limit_bytes=16 * 2**20),
        cost_estimate=pl.CostEstimate(flops=2**27, bytes_accessed=2**20, transcendentals=0),
    )(where, ids)


def spread(*refs):
    parts = refs[:-4]
    pos_ref, rows_ref, table, sems = refs[-4:]

    @pl.when(pl.program_id(0) == 0)
    def _():
        copies = []
        end = sum(part.shape[0] for part in parts)
        table[end:, :] = jnp.zeros_like(table[end:, :])
        for i, (part, start) in enumerate(zip(parts, places_of(parts))):
            copies.append(pltpu.make_async_copy(part, table.at[pl.ds(start, part.shape[0]), :], sems.at[i]))
        for copy in copies:
            copy.start()
        for copy in copies:
            copy.wait()

    rows_ref[...] = looked_up(pos_ref[...], table[...]).astype(jnp.bfloat16)


def places_of(parts):
    return [sum(part.shape[0] for part in parts[:i]) for i in range(len(parts))]


def looked_up(pos, table):
    lane = lax.broadcasted_iota(jnp.int32, pos.shape, 1)
    lanes = pos.shape[1]
    hot = [(pos == lane + start).astype(jnp.bfloat16) for start in range(0, table.shape[0], lanes)]
    return jnp.dot(jnp.concatenate(hot, axis=1), table, preferred_element_type=jnp.float32)


def spread_rows(parts, pos):
    deep, depth = late_place(ROOM), parts[0].shape[1]
    rows, lanes = 2 * KEYS, pos.shape[1]
    return pl.pallas_call(
        spread,
        grid=(pos.shape[0] // rows,),
        in_specs=[pl.BlockSpec(memory_space=pl.ANY)] * len(parts) + [pl.BlockSpec((rows, lanes), lambda i: (i, 0))],
        out_specs=pl.BlockSpec((rows, depth), lambda i: (i, 0)),
        out_shape=jax.ShapeDtypeStruct((pos.shape[0], depth), jnp.bfloat16),
        scratch_shapes=[pltpu.VMEM((deep, depth), jnp.bfloat16), pltpu.SemaphoreType.DMA((len(parts),))],
        compiler_params=pltpu.CompilerParams(vmem_limit_bytes=32 * 2**20),
        cost_estimate=pl.CostEstimate(
            flops=2 * pos.shape[0] * deep * depth, bytes_accessed=8 * 2**20, transcendentals=0
        ),
    )(*parts, pos)


def attend_last(rows_ref, near_ref, far_ref, pos_ref, gain_ref, wk, wv, q, o, enc_ref, table, *, place):
    @pl.when(pl.program_id(0) == 0)
    def _():
        table[...] = jnp.zeros_like(table)
        room = near_ref.shape[0]
        table[:room, :] = near_ref[...]
        table[room : 2 * room, :] = far_ref[...]

    wide = rows_ref[...].astype(jnp.float32) + looked_up(pos_ref[...] - place, table[...])
    enc = normed(wide, gain_ref[...])
    enc_ref[...] = enc
    span_attention(enc, wk, wv, q, o)


def attention_last(rows, near, far, pos, place, gain, w_pair, q):
    spans = pos.shape[0] // KEYS
    room, depth = near.shape
    width = w_pair.shape[1]
    keys, values = (pl.BlockSpec((depth, width), lambda i, at=at: (at, 0)) for at in range(2))
    part = pl.BlockSpec((room, depth), lambda i: (0, 0))
    tokens = pl.BlockSpec((2 * SPAN, width), lambda i: (i, 0))
    span = pl.BlockSpec((2 * KEYS, depth), lambda i: (i, 0))
    return pl.pallas_call(
        functools.partial(attend_last, place=place),
        grid=(spans // 2,),
        in_specs=[
            span,
            part,
            part,
            pl.BlockSpec((2 * KEYS, pos.shape[1]), lambda i: (i, 0)),
            pl.BlockSpec((1, depth), lambda i: (0, 0)),
            keys, values, tokens,
        ],
        out_specs=[tokens, span],
        out_shape=[
            jax.ShapeDtypeStruct((spans * SPAN, width), jnp.bfloat16),
            jax.ShapeDtypeStruct((spans * KEYS, depth), jnp.bfloat16),
        ],
        scratch_shapes=[pltpu.VMEM((-(-2 * room // LANES) * LANES, depth), jnp.bfloat16)],
        compiler_params=pltpu.CompilerParams(vmem_limit_bytes=40 * 2**20),
        cost_estimate=pl.CostEstimate(
            flops=spans * KEYS * depth * width * 5, bytes_accessed=8 * 2**20, transcendentals=spans * 2**16
        ),
    )(rows, near, far, pos, gain.reshape(1, -1), w_pair, w_pair, q)


def regroup(y_ref, w_ref, out_ref):
    pieces, sides, _, width = out_ref.shape
    for piece in range(pieces):
        for side in range(sides):
            start = pl.multiple_of((piece * sides + (side ^ y_ref[0])) * width, width)
            out_ref[piece, side] = w_ref[:, pl.ds(start, width)]


def regrouped(y, w, pieces, width):
    vmem = pl.BlockSpec(memory_space=pltpu.VMEM)
    return pl.pallas_call(
        regroup,
        in_specs=[pl.BlockSpec(memory_space=pltpu.SMEM), vmem],
        out_specs=vmem,
        out_shape=jax.ShapeDtypeStruct((pieces, 2, w.shape[0], width), w.dtype),
        compiler_params=pltpu.CompilerParams(vmem_limit_bytes=8 * 2**20),
        cost_estimate=pl.CostEstimate(flops=0, bytes_accessed=2 * w.size * 2, transcendentals=0),
    )(y.reshape(1), w)


def gather_z(x):
    n = lax.axis_size("z")
    blocks = lax.all_gather(x, "z")
    z = lax.axis_index("z")
    return [lax.dynamic_index_in_dim(blocks, lax.rem(z + n - d, n), 0, keepdims=False) for d in range(n)]


def hop(x, axis, by):
    n = lax.axis_size(axis)
    return lax.ppermute(x, axis, [(i, (i + by) % n) for i in range(n)])


def both_ways(right, left):
    return hop(right, "z", 1), hop(left, "z", -1)


def first_step(near, far):
    return tuple(jnp.concatenate(pair, axis=0) for pair in zip(both_ways(near, near), both_ways(far, far)))


def last_step(*steps):
    right, left = zip(*steps)
    half = right[-1].shape[0] // 2
    return [*right, hop(right[-1][:half], "z", 1), hop(left[-1][half:], "z", -1), *left[::-1]]


def outputs(y, near, far, blocks, ours, theirs):
    z, zs, seqs = lax.axis_index("z"), lax.axis_size("z"), lax.axis_size(SEQ)
    order = (0, 1, zs - 1, 2, zs - 2, 3, zs - 3)
    level = lax.axis_index("yhi")
    at = jnp.stack([lax.rem(z + zs - d, zs) for d in order] + [level])
    sums = projected(at, [*(blocks[d - 1 if d < zs // 2 else d] for d in order[1:]), near, far], ours, theirs)
    at = jnp.stack([lax.rem(z + zs // 2, zs), y, level])
    own, par = projected_last(at, blocks[zs // 2 - 1], blocks[zs // 2], ours, theirs, sums)
    end = slice(own.shape[0] - SPAN, None)
    onward = [(2 * i + side, 2 * i + 2 + side) for i in range(seqs - 1) for side in range(2)]
    across = [(2 * i + side, 2 * i + 3 - side) for i in range(seqs - 1) for side in range(2)]
    other = lax.ppermute(par, "ylo", SWAP)
    before = lax.ppermute(own[end], SEQ + ("ylo",), onward)
    before += lax.ppermute(par[end], SEQ + ("ylo",), across).astype(jnp.float32)
    return own, other, before


def finish(residual, own, other, before):
    shifted = own + other.astype(jnp.float32)
    return residual + jnp.concatenate([before[1:], shifted[: own.shape[0] - SPAN + 1]], axis=0)


def per_device(query, residual, nbr_ids, embed, enc_gain, w_key, w_value, w_out):
    tokens, width = query.shape
    half = tokens // 2
    y = lax.axis_index("ylo")
    z = lax.axis_index("z")
    zs = lax.axis_size("z")
    seqs = lax.axis_size(SEQ)

    mine = lax.all_to_all(regrouped(y, w_out, zs, width), "z", 0, 0, tiled=True)

    depth = w_key.shape[0]
    shares = lax.axis_size(SEQ[1:])
    each = 2 * depth // shares
    share = lax.axis_index(SEQ[1:])
    start = lax.rem(share, shares // 2) * each
    piece = jnp.where(
        share < shares // 2,
        lax.dynamic_slice_in_dim(w_key, start, each, 0),
        lax.dynamic_slice_in_dim(w_value, start, each, 0),
    )
    piece = lax.ppermute(piece, "ylo", SWAP)

    where = jnp.stack([lax.axis_index(MP), y, z]).astype(jnp.int32)
    ids, piece = lax.optimization_barrier((nbr_ids.reshape(-1, nbr_ids.shape[-1]), piece))
    slots = chosen_rows(ids, where, embed.shape[0])
    chosen = jnp.concatenate([slots[0, :ROOM], slots[8, :ROOM]])
    picked = embed.at[chosen].get(mode="promise_in_bounds")

    w_pair = lax.all_gather(piece, SEQ[1:], axis=0, tiled=True)
    got = lax.ppermute(picked[ROOM:], "ylo", SWAP)

    step1 = first_step(picked[:ROOM], got)

    ids, query, _ = lax.optimization_barrier((ids, query, got))
    pos, over = planned(ids, where, embed.shape[0], ROOM, width)
    mine = jnp.concatenate([mine.reshape(-1, width), over], axis=0)
    mine, _ = lax.optimization_barrier((mine, step1))
    ours = lax.all_gather(mine, SEQ[1:], axis=0, tiled=False)
    level = lax.ppermute(mine, "yhi", SWAP)

    following = lax.ppermute(query[:SPAN], SEQ, [(i + 1, i) for i in range(seqs - 1)])
    moved = jnp.concatenate([query[SPAN - 1 :], following[: SPAN - 1]], axis=0).reshape(2, half, width)
    step1, moved = lax.optimization_barrier((step1, moved))
    step2 = both_ways(*step1)
    q_own = lax.dynamic_index_in_dim(moved, y, 0, keepdims=False)
    q_sent = lax.dynamic_index_in_dim(moved, 1 - y, 0, keepdims=False)
    step2, q_own, q_sent, w_pair, level = lax.optimization_barrier((step2, q_own, q_sent, w_pair, level))
    theirs = lax.all_gather(level, SEQ[1:], axis=0, tiled=False)
    step3 = both_ways(*step2)
    q_par = lax.ppermute(q_sent, "ylo", SWAP)

    rights, lefts = zip(step1, step2, step3)
    rows = spread_rows([picked[:ROOM], got, *rights, *lefts[::-1]], pos)
    _, _, _, last_near, last_far, *_ = last_step(step1, step2, step3)
    a_par, enc = attention_last(rows, last_near, last_far, pos, late_place(ROOM), enc_gain, w_pair, q_par)
    a_rest = lax.ppermute(a_par, "ylo", SWAP)
    a_own = attention(enc, w_key, w_value, q_own)
    step1 = first_step(a_own, a_rest)
    step2 = both_ways(*step1)
    step3 = both_ways(*step2)
    fast = outputs(y, a_own, a_rest, last_step(step1, step2, step3), ours, theirs)

    def slow():
        enc = normed(half_rows(nbr_ids, embed, y), enc_gain)
        a_rest = lax.ppermute(attention(enc, w_pair[:depth], w_pair[depth:], q_par), "ylo", SWAP)
        a_own = attention(enc, w_key, w_value, q_own)
        blocks = gather_z(jnp.concatenate([a_own, a_rest], axis=0))
        across = blocks[zs // 2]
        blocks = [*blocks[1 : zs // 2], across[:half], across[half:], *blocks[zs // 2 + 1 :]]
        return finish(residual, *outputs(y, a_own, a_rest, blocks, ours, theirs))

    over = jnp.maximum(jnp.max(ours[:, width:, :]), jnp.max(theirs[:, width:, :])).astype(jnp.float32) > 0
    return lax.cond(over, slow, lambda: finish(residual, *fast))


def solution(mesh):
    fine = Mesh(mesh.devices.reshape(2, 4, 2, 8, 2), SEQ + MP)
    return jax.shard_map(
        per_device,
        mesh=fine,
        in_specs=(
            P(SEQ, MP),
            P(SEQ, MP),
            P(SEQ, None, None),
            P(MP, None),
            P(),
            P(None, MP),
            P(None, MP),
            P(MP + SEQ, None),
        ),
        out_specs=P(SEQ, MP),
        check_vma=False,
    )
```
